128 devices in a mesh: dp: 4 (over z), ctx: 32 (over y, x, core).
Axes of the slice: x: 4, y: 4, z: 4, core: 2. Of those that a mesh axis runs over, the one named last changes fastest.
Arguments:
- queries: bfloat16 [32768, 4096], P(('dp', 'ctx')), parts along dimension 0, may hold values from -10 to 10
- keys: bfloat16 [32768, 1024], P(('dp', 'ctx')), parts along dimension 0, may hold values from -6 to 6
- values: bfloat16 [32768, 1024], P(('dp', 'ctx')), parts along dimension 0, may hold values from -6 to 6
- doc_lengths: int32 [64], P('dp'), parts along dimension 0, may hold values from 1 to 4352, 8192 in all
Outputs:
- attended: bfloat16 [32768, 4096], P(('dp', 'ctx')), parts along dimension 0
The draws below stay inside these ranges and needn't reach their ends.
There are 4 independent parts, one for each index of `dp`. The reference program is written for one: setup_inputs(seed, part) draws one part's arguments, and reference() takes and returns one part's arrays. A program takes and returns all parts, laid end to end along the dimension named above; each array names one. Nothing has to cross between parts.
All inputs are finite; a program needn't handle non-finite values.
Results may differ from the reference program's by a relative error of at most 0.0055.
Values may be sent and summed in bfloat16 or wider, within the bound.
No kernel may reach another device: no remote copies, remote signals or barrier semaphores. Data moves between devices by JAX's collectives and lax.ppermute only.
A program may use at most 128 MiB of HBM per device.

```python
import math
import jax
import jax.numpy as jnp
import numpy as np
from jax import lax

H = 32
KVH = 8
DH = 128
SEQ = 8192
MAXDOC = 4352
DOCS = 16


def key_field(key):
    return jax.random.normal(key, (SEQ, KVH * DH), jnp.float32)


def draw_keys(key, part):
    base = key_field(key)
    drawn = jnp.clip(base, -6.0, 6.0)
    result = drawn
    return result.astype(jnp.bfloat16)


def draw_queries(key, part):
    key = jax.random.fold_in(key, 7)
    noise = jax.random.normal(key, (SEQ, H * DH), jnp.float32)
    drawn = jnp.clip(noise, -6.0, 6.0)
    result = drawn
    return result.astype(jnp.bfloat16)


def block_scale(key, dims, pieces, smallest, high):
    def one(axis_at, blocks):
        draws = jax.random.uniform(jax.random.fold_in(jax.random.fold_in(key, 6), axis_at), (blocks,), jnp.float32, smallest / len(pieces), high / len(pieces))
        return jnp.repeat(jnp.exp(draws), dims[axis_at] // blocks).reshape((-1,) + (1,) * (len(dims) - axis_at - 1))

    level = one(*pieces[0])
    for cut in pieces[1:]:
        level = level * one(*cut)
    return level


def length_profile(amount, total, reach, lean):
    weights = [(1 << 20) // math.isqrt(standing ** lean) + 1 for standing in range(2, amount + 1)]
    spare, holding = total - reach - (amount - 1), [1] * (amount - 1)
    while spare > 0:
        candidates = [i for i in range(amount - 1) if holding[i] < reach]
        whole, left = sum([weights[i] for i in candidates]), spare
        for i in candidates:
            addition = min(reach - holding[i], max(1, left * weights[i] // whole), spare)
            holding[i] = holding[i] + addition
            spare = spare - addition
    return np.array([reach] + holding)


def ragged_sizes(own_key, amount, total, reach, skew):
    if amount == 2:
        one = jax.random.randint(own_key, (), max(1, total - reach), min(reach, total - 1) + 1)
        return jnp.stack([one, total - one])
    sizes = jnp.asarray(length_profile(amount, total, reach, skew), jnp.int32)
    couples = (amount - 1) // 2
    source_of, receiver = sizes[1:1 + 2 * couples:2], sizes[2:2 + 2 * couples:2]
    room = jnp.minimum(source_of - 1, reach - receiver)
    moved = jax.random.randint(jax.random.fold_in(own_key, 1), (couples,), 0, 1 << 20) % (room + 1)
    sizes = sizes.at[1:1 + 2 * couples:2].set(source_of - moved).at[2:2 + 2 * couples:2].set(receiver + moved)
    return sizes[jax.random.permutation(jax.random.fold_in(own_key, 2), amount)]


def normal_values(rng, shape, scale, reach, shards=(), kind=jnp.bfloat16):
    level = block_scale(rng, shape, shards, -0.22, 0.18) if shards else 1.0
    array = jax.random.normal(rng, shape, jnp.float32) * scale * level
    return jnp.minimum(jnp.maximum(array, -reach), reach).astype(kind)


def setup_inputs(seed: int = 0, part: int = 0) -> dict:
    splits = jax.random.split(jax.random.key(seed), 5)
    part_splits = jax.random.split(jax.random.fold_in(splits[4], part), 5)
    return {
        "queries": draw_queries(jax.random.fold_in(jax.random.fold_in(splits[4], part), 71), part),
        "keys": draw_keys(jax.random.fold_in(jax.random.fold_in(splits[4], part), 71), part),
        "values": normal_values(part_splits[2], (SEQ, KVH * DH), 1.0, 6.0, ((0, 32),)),
        "doc_lengths": ragged_sizes(part_splits[3], DOCS, SEQ, MAXDOC, 2).astype(jnp.int32),
    }


NEG_FILL = -1e+30

def pick_rows(row_count):
    for tile_rows in (512, 256, 128, 64, 32, 16, 8, 4, 2, 1):
        if row_count % tile_rows == 0:
            return tile_rows
    return 1

def doc_firsts(doc_lengths, count):
    doc_end = jnp.cumsum(doc_lengths).astype(jnp.int32)
    doc_first = (doc_end - doc_lengths).astype(jnp.int32)
    positions = jnp.arange(count, dtype=jnp.int32)
    inside = (doc_first[None, :] <= positions[:, None]) & (positions[:, None] < doc_end[None, :])
    return lax.optimization_barrier(jnp.sum(jnp.where(inside, doc_first[None, :], 0), axis=1)).astype(jnp.int32)

def tile_update(carry, q_block, k_tile, v_tile, q_pos, q_first, k_pos, scaling):
    running_max, totals, summed = carry
    scores = jnp.einsum('qkgd,rkd->kgqr', q_block.astype(jnp.float32), k_tile.astype(jnp.float32)) * scaling
    visible = (k_pos[None, :] <= q_pos[:, None]) & (k_pos[None, :] >= q_first[:, None])
    scores = jnp.where(visible, scores, NEG_FILL)
    new_max = jnp.maximum(running_max, lax.optimization_barrier(jnp.max(scores, axis=-1)))
    weights = jnp.where(visible, jnp.exp(scores - new_max[..., None]), 0.0)
    rescale = jnp.exp(running_max - new_max)
    totals = totals * rescale + lax.optimization_barrier(jnp.sum(weights, axis=-1))
    rounded = lax.optimization_barrier(weights.astype(jnp.bfloat16)).astype(jnp.float32)
    summed = summed * rescale[..., None] + jnp.einsum('kgqr,rkd->kgqd', rounded, v_tile.astype(jnp.float32))
    return (new_max, totals, summed)

def reference(queries, keys, values, doc_lengths):
    seq_rows = queries.shape[0]
    block = pick_rows(seq_rows)
    q_per_kv = H // KVH
    scaling = 1.0 / math.sqrt(DH)
    doc_first = doc_firsts(doc_lengths, seq_rows)
    query_heads = queries.reshape(seq_rows, KVH, q_per_kv, DH)
    key_heads = keys.reshape(seq_rows, KVH, DH)
    value_heads = values.reshape(seq_rows, KVH, DH)

    def one_block(block_id):
        opening_row = (block_id * block).astype(jnp.int32)
        q_block = lax.dynamic_slice_in_dim(query_heads, opening_row, block, 0)
        q_pos = opening_row + jnp.arange(block, dtype=jnp.int32)
        q_first = lax.dynamic_slice_in_dim(doc_first, opening_row, block, 0)
        opening_tile = (q_first[0] // block).astype(jnp.int32)
        start_carry = (jnp.full((KVH, q_per_kv, block), NEG_FILL, jnp.float32), jnp.zeros((KVH, q_per_kv, block), jnp.float32), jnp.zeros((KVH, q_per_kv, block, DH), jnp.float32))

        def advance(tile_id, carry):
            key_row = (tile_id * block).astype(jnp.int32)
            k_tile = lax.dynamic_slice_in_dim(key_heads, key_row, block, 0)
            v_tile = lax.dynamic_slice_in_dim(value_heads, key_row, block, 0)
            k_pos = key_row + jnp.arange(block, dtype=jnp.int32)
            return tile_update(carry, q_block, k_tile, v_tile, q_pos, q_first, k_pos, scaling)
        running_max, totals, summed = lax.fori_loop(opening_tile, (block_id + 1).astype(jnp.int32), advance, start_carry)
        result = summed / totals[..., None]
        return jnp.transpose(result, (2, 0, 1, 3)).reshape(block, H * DH).astype(jnp.bfloat16)
    blocks_out = lax.map(one_block, jnp.arange(seq_rows // block, dtype=jnp.int32))
    return blocks_out.reshape(seq_rows, H * DH)
```

```python
import functools
import math

import jax
import jax.numpy as jnp
from jax import lax
from jax.experimental import pallas as pl
from jax.experimental.pallas import tpu as pltpu
from jax.sharding import PartitionSpec as P

H = 32
KVH = 8
DH = 128
QPK = H // KVH
GROUP = QPK * DH

YS = 4
XS = 4
CS = 2

SMALL = 256
BIG = 512
NEG_FILL = -1e30
LOG2_SCALE = math.log2(math.e) / math.sqrt(DH)


def ctx_index(y, x, c):
    return ((y % YS) * XS + x % XS) * CS + c % CS


def shift(dy, dx, dc):
    return [
        (ctx_index(y, x, c), ctx_index(y + dy, x + dx, c + dc))
        for y in range(YS)
        for x in range(XS)
        for c in range(CS)
    ]


def head_groups():
    return [[ctx_index(y, x, c) for y in range(YS) for c in range(CS)] for x in range(XS)]


def doc_firsts(doc_lengths, count):
    doc_end = jnp.cumsum(doc_lengths)
    doc_first = doc_end - doc_lengths
    positions = jnp.arange(count, dtype=jnp.int32)
    inside = (doc_first[None, :] <= positions[:, None]) & (positions[:, None] < doc_end[None, :])
    return jnp.sum(jnp.where(inside, doc_first[None, :], 0), axis=1)


def attend_kernel(pieces, rows, places, bounds, first, *refs):
    q_refs = refs[:pieces]
    kv_own, kv_a, kv_b, kv_c, kv_d = refs[pieces : pieces + 5]
    o_refs = refs[pieces + 5 : 2 * pieces + 5]
    k_all, v_all, q_all, acc, top, sems = refs[2 * pieces + 5 :]

    run = XS * 0 + 2 * rows
    copies = []

    def bring(part, place, ys, y_from):
        for i in range(ys):
            src = pl.ds(i * run, run)
            dst = pl.ds(pl.multiple_of(((y_from + i) * XS + place) * run, run), run)
            n = len(copies)
            copies.append(
                pltpu.make_async_copy(part.at[src, pl.ds(0, DH)], k_all.at[dst, :], sems.at[n])
            )
            copies.append(
                pltpu.make_async_copy(
                    part.at[src, pl.ds(DH, DH)], v_all.at[dst, pl.ds(0, DH)], sems.at[n + 1]
                )
            )

    bring(kv_own, places[0], YS, 0)
    bring(kv_a, places[1], YS, 0)
    bring(kv_b, places[2], YS, 0)
    bring(kv_c, places[3], YS // 2, 0)
    bring(kv_d, places[3], YS // 2, YS // 2)
    for copy in copies:
        copy.start()
    v_all[:, DH:] = jnp.ones((v_all.shape[0], DH), v_all.dtype)
    for copy in copies:
        copy.wait()

    def tile(p, key_row, size, masked):
        key_row = pl.multiple_of(key_row, SMALL)
        k_tile = k_all[pl.ds(key_row, size), :]
        v_tile = v_all[pl.ds(key_row, size), :]
        if masked:
            k_pos = key_row + lax.broadcasted_iota(jnp.int32, (rows, size), 1)
            q_pos = bounds[p, 4] + lax.broadcasted_iota(jnp.int32, (rows, size), 0)
            visible = (k_pos <= q_pos) & (k_pos >= first[p * rows : (p + 1) * rows, :])
        for h in range(QPK):
            at = slice(h * rows, (h + 1) * rows)
            scores = lax.dot_general(
                q_all[at, :], k_tile, (((1,), (1,)), ((), ())), preferred_element_type=jnp.float32
            )
            scores = scores * LOG2_SCALE
            if masked:
                scores = jnp.where(visible, scores, NEG_FILL)
            old = top[at, :]
            new = jnp.maximum(old, jnp.max(scores, axis=1, keepdims=True))
            weights = jnp.exp2(scores - jnp.tile(new, (1, size // DH)))
            rescale = jnp.exp2(old - new)
            top[at, :] = new
            acc[at, :] = acc[at, :] * jnp.tile(rescale, (1, 2)) + jnp.dot(
                weights.astype(jnp.bfloat16), v_tile, preferred_element_type=jnp.float32
            )

    for p in range(pieces):
        for h in range(QPK):
            q_all[h * rows : (h + 1) * rows, :] = q_refs[p][:, h * DH : (h + 1) * DH]
        top[...] = jnp.full(top.shape, NEG_FILL, top.dtype)
        acc[...] = jnp.zeros(acc.shape, acc.dtype)
        lo, mid, last, hi = bounds[p, 0], bounds[p, 1], bounds[p, 2], bounds[p, 3]

        @pl.loop(lo, mid)
        def _(t):
            tile(p, t * SMALL, SMALL, True)

        bigs = jnp.maximum(last - mid, 0) // (BIG // SMALL)

        @pl.loop(0, bigs)
        def _(t):
            tile(p, mid * SMALL + t * BIG, BIG, False)

        @pl.loop(mid + bigs * (BIG // SMALL), hi)
        def _(t):
            tile(p, t * SMALL, SMALL, True)

        for h in range(QPK):
            at = slice(h * rows, (h + 1) * rows)
            o_refs[p][:, h * DH : (h + 1) * DH] = (acc[at, :DH] / acc[at, DH:]).astype(jnp.bfloat16)


def attend(places, bounds, first, q_pieces, kv_parts):
    pieces = len(q_pieces)
    rows = q_pieces[0].shape[0]
    seq = rows * YS * XS * CS
    vmem = pl.BlockSpec(memory_space=pltpu.VMEM)
    smem = pl.BlockSpec(memory_space=pltpu.SMEM)
    return pl.pallas_call(
        functools.partial(attend_kernel, pieces, rows),
        out_shape=[jax.ShapeDtypeStruct((rows, GROUP), jnp.bfloat16)] * pieces,
        in_specs=[smem, smem, vmem] + [vmem] * pieces + [pl.BlockSpec(memory_space=pl.ANY)] * 5,
        out_specs=[vmem] * pieces,
        scratch_shapes=[
            pltpu.VMEM((seq, DH), jnp.bfloat16),
            pltpu.VMEM((seq, 2 * DH), jnp.bfloat16),
            pltpu.VMEM((QPK * rows, DH), jnp.bfloat16),
            pltpu.VMEM((QPK * rows, 2 * DH), jnp.float32),
            pltpu.VMEM((QPK * rows, DH), jnp.float32),
            pltpu.SemaphoreType.DMA((8 * YS,)),
        ],
        compiler_params=pltpu.CompilerParams(vmem_limit_bytes=40 * 1024 * 1024),
        cost_estimate=pl.CostEstimate(
            flops=pieces * 4 * QPK * rows * seq // 4 * DH,
            bytes_accessed=8 * 1024 * 1024,
            transcendentals=pieces * QPK * rows * seq // 4,
        ),
    )(places, bounds, first, *q_pieces, *kv_parts)


def piece_facts(doc_first, starts, rows):
    bounds, firsts = [], []
    for start in starts:
        first = lax.dynamic_slice_in_dim(doc_first, start, rows, 0)
        lo = first[0] // SMALL
        hi = (start + rows) // SMALL
        mid = jnp.minimum((first[rows - 1] + SMALL - 1) // SMALL, hi)
        last = start // SMALL
        bounds.append(jnp.stack([lo, mid, last, hi, start]))
        firsts.append(first)
    return jnp.stack(bounds).astype(jnp.int32), jnp.concatenate(firsts)[:, None]


def per_device(queries, keys, values, doc_lengths):
    rows = queries.shape[0]
    seq = rows * YS * XS * CS
    rank = lax.axis_index("ctx")
    c, x, y = rank % CS, (rank // CS) % XS, rank // (CS * XS)

    pairs = jnp.concatenate(
        [keys.reshape(rows, KVH, DH), values.reshape(rows, KVH, DH)], axis=2
    )
    pairs = jnp.transpose(pairs, (1, 0, 2))
    own = lax.all_to_all(
        pairs, "ctx", split_axis=0, concat_axis=0, tiled=True, axis_index_groups=head_groups()
    ).reshape(YS * CS * rows, 2 * DH)
    half = YS * CS * rows // 2
    part_a = lax.ppermute(own, "ctx", shift(0, 1, 0))
    part_b = lax.ppermute(own, "ctx", shift(0, XS - 1, 0))
    part_c = lax.ppermute(part_a[:half], "ctx", shift(0, 1, 0))
    part_d = lax.ppermute(part_b[half:], "ctx", shift(0, XS - 1, 0))
    kv_parts = (own, part_a, part_b, part_c, part_d)
    places = jnp.stack([x, (x + XS - 1) % XS, (x + 1) % XS, (x + 2) % XS]).astype(jnp.int32)

    queries, _ = lax.optimization_barrier((queries, own))
    doc_first = doc_firsts(doc_lengths, seq)

    def columns(dy, dc):
        return (((y + dy) % YS) * CS + (c + dc) % CS) * GROUP

    def fetch(dy, dc):
        part = lax.dynamic_slice_in_dim(queries, columns(dy, dc), GROUP, 1)
        return part if dy == 0 and dc == 0 else lax.ppermute(part, "ctx", shift(dy, 0, dc))

    steps = [(1, 0), (1, 1), (3, 0), (3, 1), (2, 0), (2, 1), (0, 1), (0, 0)]
    got = [fetch(dy, dc) for dy, dc in steps]
    starts = [
        (((y + YS - dy) % YS * XS + x) * CS + (c + dc) % CS) * rows for dy, dc in steps
    ]
    out = jnp.zeros((rows, H * DH), jnp.bfloat16)
    for begin in range(0, len(steps), CHUNK):
        take = slice(begin, begin + CHUNK)
        bounds, first = piece_facts(doc_first, starts[take], rows)
        done = attend(places, bounds, first, got[take], kv_parts)
        for (dy, dc), piece in zip(steps[take], done, strict=True):
            if dy or dc:
                piece = lax.ppermute(piece, "ctx", shift(YS - dy, 0, dc))
            out = lax.dynamic_update_slice(out, piece, (0, columns(dy, dc)))
    return out


CHUNK = 4


def solution(mesh):
    placed = (P(("dp", "ctx"), None), P(("dp", "ctx"), None), P(("dp", "ctx"), None), P("dp"))
    return jax.shard_map(
        per_device, mesh=mesh, in_specs=placed, out_specs=P(("dp", "ctx"), None), check_vma=False
    )
```

```python
import functools
import math

import jax
import jax.numpy as jnp
from jax import lax
from jax.experimental import pallas as pl
from jax.experimental.pallas import tpu as pltpu
from jax.sharding import PartitionSpec as P

H = 32
KVH = 8
DH = 128
QPK = H // KVH
GROUP = QPK * DH

YS = 4
XS = 4
CS = 2

UNIT = 256
TAIL = 512
WIDE = 2048
STACK = 512
MARK = 128.0
NEG_FILL = -1e30
LOG2_SCALE = math.log2(math.e) / math.sqrt(DH)


STEPS = [(dy, dc) for dc in range(CS) for dy in range(YS)]


def ctx_index(y, x, c):
    return ((y % YS) * XS + x % XS) * CS + c % CS


def shift(dy, dx, dc):
    return [
        (ctx_index(y, x, c), ctx_index(y + dy, x + dx, c + dc))
        for y in range(YS)
        for x in range(XS)
        for c in range(CS)
    ]


def head_groups():
    return [[ctx_index(y, x, c) for y in range(YS) for c in range(CS)] for x in range(XS)]


def place(rank):
    return rank >> 3, (rank >> 1) & (XS - 1), rank & (CS - 1)


def group_at(y, c, dy, dc):
    return (((y + dy) & (YS - 1)) << 1) + (c ^ dc)


def split_kernel(rank, queries, keys, values, k_out, v_out, *q_out):
    y, _, c = place(rank[0])
    for h in range(KVH):
        k_out[h] = keys[:, h * DH : (h + 1) * DH]
        v_out[h] = values[:, h * DH : (h + 1) * DH]
    for (dy, dc), out in zip(STEPS, q_out, strict=True):
        column = pl.multiple_of(group_at(y, c, dy, dc) * GROUP, GROUP)
        out[...] = queries[:, pl.ds(column, GROUP)]


def split(rank, queries, keys, values):
    rows = queries.shape[0]
    vmem = pl.BlockSpec(memory_space=pltpu.VMEM)
    by_head = jax.ShapeDtypeStruct((KVH, rows, DH), jnp.bfloat16)
    return pl.pallas_call(
        split_kernel,
        out_shape=[by_head] * 2 + [jax.ShapeDtypeStruct((rows, GROUP), jnp.bfloat16)] * len(STEPS),
        in_specs=[pl.BlockSpec(memory_space=pltpu.SMEM)] + [vmem] * 3,
        out_specs=[vmem] * (2 + len(STEPS)),
    )(rank, queries, keys, values)


def join_kernel(rank, *refs):
    pieces, out, sems = refs[: len(STEPS)], refs[-2], refs[-1]
    y, _, c = place(rank[0])
    copies = []
    for i, (dy, dc) in enumerate(STEPS):
        column = pl.multiple_of(group_at(y, c, dy, dc) * GROUP, GROUP)
        copies.append(
            pltpu.make_async_copy(pieces[i], out.at[:, pl.ds(column, GROUP)], sems.at[i])
        )
    for copy in copies:
        copy.start()
    for copy in copies:
        copy.wait()


def join(rank, pieces):
    vmem = pl.BlockSpec(memory_space=pltpu.VMEM)
    return pl.pallas_call(
        join_kernel,
        out_shape=jax.ShapeDtypeStruct((pieces[0].shape[0], H * DH), jnp.bfloat16),
        in_specs=[pl.BlockSpec(memory_space=pltpu.SMEM)] + [vmem] * len(pieces),
        out_specs=pl.BlockSpec(memory_space=pl.ANY),
        scratch_shapes=[pltpu.SemaphoreType.DMA((len(pieces),))],
    )(rank, *pieces)


def attend_kernel(pieces, dc, rank, doc_lengths, marks, keys, values, *refs):
    q_refs, o_refs = refs[:pieces], refs[pieces : 2 * pieces]
    q_all, o_all, acc, top = refs[2 * pieces :]
    rows = UNIT
    y, x, c = place(rank[0])

    for p in range(pieces):
        for h in range(QPK):
            q_all[p, h * rows : (h + 1) * rows, :DH] = q_refs[p][:, h * DH : (h + 1) * DH]

    def tile(p, start, key_tile, size, hidden):
        at_key = pl.ds(pl.multiple_of(key_tile * UNIT, UNIT), size)
        k_tile = jnp.concatenate([keys[at_key, :], marks[at_key, :]], axis=1)
        v_tile = jnp.concatenate([values[at_key, :], jnp.ones((size, DH), jnp.bfloat16)], axis=1)
        count = QPK * rows // STACK
        stacks = [slice(i * STACK, (i + 1) * STACK) for i in range(count)]

        def multiply(i):
            return lax.dot_general(
                q_all[p, stacks[i], :],
                k_tile,
                (((1,), (1,)), ((), ())),
                preferred_element_type=jnp.float32,
            )

        def weigh(i, scores):
            if hidden:
                ahead = key_tile * UNIT + size - hidden - start
                q_row = lax.broadcasted_iota(jnp.int32, (STACK, hidden), 0) % rows - ahead
                keep = lax.broadcasted_iota(jnp.int32, (STACK, hidden), 1) <= q_row
                last = jnp.where(keep, scores[:, size - hidden :], NEG_FILL)
                if hidden == size:
                    scores = last
                else:
                    scores = jnp.concatenate([scores[:, : size - hidden], last], axis=1)
            old = top[stacks[i], :]
            new = jnp.maximum(old, jnp.max(scores, axis=1, keepdims=True))
            weights = jnp.exp2((scores - jnp.tile(new, (1, size // DH))) * LOG2_SCALE)
            top[stacks[i], :] = new
            return weights.astype(jnp.bfloat16), jnp.exp2((old - new) * LOG2_SCALE)

        def add(i, weights, rescale):
            acc[stacks[i], :] = acc[stacks[i], :] * jnp.tile(rescale, (1, 2)) + jnp.dot(
                weights, v_tile, preferred_element_type=jnp.float32
            )

        coming, ready = multiply(0), None
        for i in range(count):
            scores = coming
            if i + 1 < count:
                coming = multiply(i + 1)
            weighed = weigh(i, scores)
            if ready is not None:
                add(i - 1, *ready)
            ready = weighed
        add(count - 1, *ready)

    @pl.loop(0, pieces)
    def _(p):
        start = ((((y - p) & (YS - 1)) * XS + x) * CS + (c ^ dc)) * rows

        def document(d, so_far):
            first, end = so_far
            after = end + doc_lengths[d]
            return jnp.where(end <= start, end, first), after

        first, _ = lax.fori_loop(0, doc_lengths.shape[0], document, (0, 0), unroll=True)
        lo, hi = first // UNIT, start // UNIT + 1
        mark = marks[pl.ds(pl.multiple_of(start, UNIT), rows), :]
        for h in range(QPK):
            q_all[p, h * rows : (h + 1) * rows, DH:] = mark + mark
        top[...] = jnp.full(top.shape, NEG_FILL, top.dtype)
        acc[...] = jnp.zeros(acc.shape, acc.dtype)

        tail, wide = TAIL // UNIT, WIDE // UNIT
        rest = jnp.maximum(hi - tail - lo, 0)
        odd = rest % tail
        begin = lo + odd
        wides = (rest - odd) // wide
        alone = jnp.where(hi == 1, 1, odd)

        @pl.loop(0, alone)
        def _(t):
            tile(p, start, lo, UNIT, UNIT)

        @pl.loop(0, wides)
        def _(t):
            tile(p, start, begin + t * wide, WIDE, 0)

        @pl.loop(0, (rest - odd - wides * wide) // tail)
        def _(t):
            tile(p, start, begin + wides * wide + t * tail, TAIL, 0)

        @pl.when(hi > 1)
        def _():
            tile(p, start, hi - tail, TAIL, UNIT)

        for h in range(QPK):
            at = slice(h * rows, (h + 1) * rows)
            o_all[p, :, h * DH : (h + 1) * DH] = (acc[at, :DH] / acc[at, DH:]).astype(jnp.bfloat16)

    for p in range(pieces):
        o_refs[p][...] = o_all[p]


def attend(dc, rank, doc_lengths, marks, keys, values, q_pieces):
    pieces = len(q_pieces)
    seq = keys.shape[0]
    vmem = pl.BlockSpec(memory_space=pltpu.VMEM)
    smem = pl.BlockSpec(memory_space=pltpu.SMEM)
    return pl.pallas_call(
        functools.partial(attend_kernel, pieces, dc),
        out_shape=[jax.ShapeDtypeStruct((UNIT, GROUP), jnp.bfloat16)] * pieces,
        in_specs=[smem] * 2 + [vmem] * (3 + pieces),
        out_specs=[vmem] * pieces,
        scratch_shapes=[
            pltpu.VMEM((pieces, QPK * UNIT, 2 * DH), jnp.bfloat16),
            pltpu.VMEM((pieces, UNIT, GROUP), jnp.bfloat16),
            pltpu.VMEM((QPK * UNIT, 2 * DH), jnp.float32),
            pltpu.VMEM((QPK * UNIT, DH), jnp.float32),
        ],
        compiler_params=pltpu.CompilerParams(vmem_limit_bytes=40 * 1024 * 1024),
        cost_estimate=pl.CostEstimate(
            flops=pieces * 4 * QPK * UNIT * seq // 4 * DH,
            bytes_accessed=8 * 1024 * 1024,
            transcendentals=pieces * QPK * UNIT * seq // 4,
        ),
    )(rank, doc_lengths, marks, keys, values, *q_pieces)


def per_device(queries, keys, values, doc_lengths):
    rows = queries.shape[0]
    seq = rows * YS * XS * CS
    run = CS * rows
    rank = lax.axis_index("ctx").astype(jnp.int32)
    y, x, c = place(rank)
    rank = rank[None]

    keys, values, *sent = split(rank, queries, keys, values)
    sent = dict(zip(STEPS, sent, strict=True))

    def to_heads(part):
        return lax.all_to_all(
            part, "ctx", split_axis=0, concat_axis=0, tiled=True, axis_index_groups=head_groups()
        ).reshape(YS, run, DH)

    def along(part, dx):
        return lax.ppermute(part, "ctx", shift(0, dx, 0))

    k_own = to_heads(keys)
    doc_lengths, values, k_own = lax.optimization_barrier((doc_lengths, values, k_own))
    k_left, k_right = along(k_own, 1), along(k_own, XS - 1)
    v_own = to_heads(values)
    v_left, v_right = along(v_own, 1), along(v_own, XS - 1)

    def send(dy, dc):
        part = sent[dy, dc]
        return lax.ppermute(part, "ctx", shift(dy, 0, dc)) if dy or dc else part

    sent, k_left, k_right = lax.optimization_barrier((sent, k_left, k_right))
    got = {(dy, 0): send(dy, 0) for dy in range(YS)}
    k_left, k_right, v_left, v_right = lax.optimization_barrier(
        (k_left, k_right, v_left, v_right)
    )
    k_far, v_far = along(k_left, 1), along(v_right, XS - 1)
    sent, got, k_far, v_far = lax.optimization_barrier((sent, got, k_far, v_far))
    got |= {(dy, 1): send(dy, 1) for dy in range(YS)}

    doc_end = jnp.cumsum(doc_lengths)
    doc_first = doc_end - doc_lengths
    positions = jnp.arange(seq, dtype=jnp.int32)[:, None]
    inside = (doc_first[None, :] <= positions) & (positions < doc_end[None, :])
    marks = jnp.where(inside, MARK, 0.0).astype(jnp.bfloat16)
    marks = jnp.pad(marks, ((0, 0), (0, DH - marks.shape[1])))

    def in_order(own, left, right, far):
        whole = jnp.zeros((YS, XS, run, DH), jnp.bfloat16)
        for part, dx in ((own, 0), (left, XS - 1), (right, 1), (far, 2)):
            at = ((x + dx) & (XS - 1)).astype(jnp.uint32)
            zero = jnp.uint32(0)
            whole = lax.dynamic_update_slice(whole, part[:, None], (zero, at, zero, zero))
        return whole.reshape(seq, DH)

    k_all = in_order(k_own, k_left, k_right, k_far)
    v_all = in_order(v_own, v_left, v_right, v_far)

    outs = []
    for dc in range(CS):
        pieces = [got[dy, dc] for dy in range(YS)]
        done = attend(dc, rank, doc_lengths, marks, k_all, v_all, pieces)
        for dy, piece in enumerate(done):
            if dy or dc:
                piece = lax.ppermute(piece, "ctx", shift(YS - dy, 0, dc))
            outs.append(piece)
    return join(rank, outs)


def solution(mesh):
    placed = (P(("dp", "ctx"), None), P(("dp", "ctx"), None), P(("dp", "ctx"), None), P("dp"))
    return jax.shard_map(
        per_device, mesh=mesh, in_specs=placed, out_specs=P(("dp", "ctx"), None), check_vma=False
    )
```

```python
import functools
import math

import jax
import jax.numpy as jnp
from jax import lax
from jax.experimental import pallas as pl
from jax.experimental.pallas import tpu as pltpu
from jax.sharding import PartitionSpec as P

H = 32
KVH = 8
DH = 128
QPK = H // KVH
GROUP = QPK * DH

YS = 4
XS = 4
CS = 2

UNIT = 256
TAIL = 512
WIDE = 2048
STACK = 512
MARK = 128.0
NEG_FILL = -1e30
LOG2_SCALE = math.log2(math.e) / math.sqrt(DH)


FAR = ((2, 0, YS // 2), (2, YS // 2, YS // 2))
PARTS = {"near": ((0, 0, YS), (XS - 1, 0, YS), (1, 0, YS)), "far": FAR}
PARTS["all"] = PARTS["near"] + FAR
STEPS = [(dy, dc) for dc in range(CS) for dy in range(YS)]


def ctx_index(y, x, c):
    return ((y % YS) * XS + x % XS) * CS + c % CS


def shift(dy, dx, dc):
    return [
        (ctx_index(y, x, c), ctx_index(y + dy, x + dx, c + dc))
        for y in range(YS)
        for x in range(XS)
        for c in range(CS)
    ]


def head_groups():
    return [[ctx_index(y, x, c) for y in range(YS) for c in range(CS)] for x in range(XS)]


def place(rank):
    return rank >> 3, (rank >> 1) & (XS - 1), rank & (CS - 1)


def group_at(y, c, dy, dc):
    return (((y + dy) & (YS - 1)) << 1) + (c ^ dc)


def vmem_call(kernel, out_shape, rank, *arrays):
    vmem = pl.BlockSpec(memory_space=pltpu.VMEM)
    return pl.pallas_call(
        kernel,
        out_shape=out_shape,
        in_specs=[pl.BlockSpec(memory_space=pltpu.SMEM)] + [vmem] * len(arrays),
        out_specs=[vmem] * len(out_shape),
    )(rank, *arrays)


def split_kernel(_, keys, values, out):
    for h in range(KVH):
        out[h, 0] = keys[:, h * DH : (h + 1) * DH]
        out[h, 1] = values[:, h * DH : (h + 1) * DH]


def query_kernel(rank, queries, *out):
    y, _, c = place(rank[0])
    for (dy, dc), part in zip(STEPS, out, strict=True):
        column = pl.multiple_of(group_at(y, c, dy, dc) * GROUP, GROUP)
        part[...] = queries[:, pl.ds(column, GROUP)]


def attend_kernel(pieces, dc, which, rank, doc_lengths, marks, *refs):
    parts = PARTS[which]
    part_refs, refs = refs[: len(parts)], refs[len(parts) :]
    q_refs, refs = refs[:pieces], refs[pieces:]
    if which == "far":
        acc_in, top_in, *refs = refs
    if which == "near":
        acc_out, top_out, *refs = refs
    else:
        o_refs, refs = refs[:pieces], refs[pieces:]
    q_all, o_all, acc, top, keys, values, *refs = refs
    rows = UNIT
    y, x, c = place(rank[0])

    for (dx, first_y, ys), part in zip(parts, part_refs, strict=True):
        at_x = (x + dx) & (XS - 1)
        for i in range(ys):
            for core in range(CS):
                block = first_y + i if which == "far" else (first_y + i) * XS + at_x
                at = pl.ds(pl.multiple_of((block * CS + core) * rows, rows), rows)
                keys[at, :] = part[i, core, 0]
                values[at, :] = part[i, core, 1]
    if which == "near":
        (near_marks,) = refs
        near_marks[...] = marks[...]
        for i in range(YS):
            at = pl.multiple_of((i * XS + ((x + 2) & (XS - 1))) * TAIL, TAIL)
            for whole in (near_marks, keys, values):
                whole[pl.ds(at, TAIL), :] = jnp.zeros((TAIL, DH), jnp.bfloat16)
        marks = near_marks

    for p in range(pieces):
        for h in range(QPK):
            q_all[p, h * rows : (h + 1) * rows, :DH] = q_refs[p][:, h * DH : (h + 1) * DH]

    def tile(p, start, first_key, size, hidden, at_row=None):
        at_key = pl.ds(pl.multiple_of(first_key if at_row is None else at_row, UNIT), size)
        at_mark = pl.ds(pl.multiple_of(first_key, UNIT), size)
        k_tile = jnp.concatenate([keys[at_key, :], marks[at_mark, :]], axis=1)
        v_tile = jnp.concatenate([values[at_key, :], jnp.ones((size, DH), jnp.bfloat16)], axis=1)
        count = QPK * rows // STACK
        stacks = [slice(i * STACK, (i + 1) * STACK) for i in range(count)]

        def multiply(i):
            return lax.dot_general(
                q_all[p, stacks[i], :],
                k_tile,
                (((1,), (1,)), ((), ())),
                preferred_element_type=jnp.float32,
            )

        def weigh(i, scores):
            if hidden:
                ahead = first_key + size - hidden - start
                q_row = lax.broadcasted_iota(jnp.int32, (STACK, hidden), 0) % rows - ahead
                keep = lax.broadcasted_iota(jnp.int32, (STACK, hidden), 1) <= q_row
                last = jnp.where(keep, scores[:, size - hidden :], NEG_FILL)
                if hidden == size:
                    scores = last
                else:
                    scores = jnp.concatenate([scores[:, : size - hidden], last], axis=1)
            old = top[stacks[i], :]
            new = jnp.maximum(old, jnp.max(scores, axis=1, keepdims=True))
            weights = jnp.exp2((scores - jnp.tile(new, (1, size // DH))) * LOG2_SCALE)
            top[stacks[i], :] = new
            return weights.astype(jnp.bfloat16), jnp.exp2((old - new) * LOG2_SCALE)

        def add(i, weights, rescale):
            acc[stacks[i], :] = acc[stacks[i], :] * jnp.tile(rescale, (1, 2)) + jnp.dot(
                weights, v_tile, preferred_element_type=jnp.float32
            )

        coming, ready = multiply(0), None
        for i in range(count):
            scores = coming
            if i + 1 < count:
                coming = multiply(i + 1)
            weighed = weigh(i, scores)
            if ready is not None:
                add(i - 1, *ready)
            ready = weighed
        add(count - 1, *ready)

    @pl.loop(0, pieces)
    def _(p):
        start = ((((y - p) & (YS - 1)) * XS + x) * CS + (c ^ dc)) * rows

        def document(d, so_far):
            first, end = so_far
            after = end + doc_lengths[d]
            return jnp.where(end <= start, end, first), after

        first, _ = lax.fori_loop(0, doc_lengths.shape[0], document, (0, 0), unroll=True)
        mark = marks[pl.ds(pl.multiple_of(start, UNIT), rows), :]
        for h in range(QPK):
            q_all[p, h * rows : (h + 1) * rows, DH:] = mark + mark

        if which == "far":
            top[...] = top_in[p]
            acc[...] = acc_in[p]

            @pl.loop(0, YS)
            def _(at_y):
                key = (at_y * XS + ((x + 2) & (XS - 1))) * TAIL

                @pl.when((key < start) & (key + TAIL > first))
                def _():
                    tile(p, start, key, TAIL, 0, at_y * TAIL)

        else:
            top[...] = jnp.full(top.shape, NEG_FILL, top.dtype)
            acc[...] = jnp.zeros(acc.shape, acc.dtype)

            lo, hi = first // UNIT, start // UNIT + 1
            tail, wide = TAIL // UNIT, WIDE // UNIT
            rest = jnp.maximum(hi - tail - lo, 0)
            odd = rest % tail
            begin = lo + odd
            wides = (rest - odd) // wide
            alone = jnp.where(hi == 1, 1, odd)

            @pl.loop(0, alone)
            def _(t):
                tile(p, start, lo * UNIT, UNIT, UNIT)

            @pl.loop(0, wides)
            def _(t):
                tile(p, start, (begin + t * wide) * UNIT, WIDE, 0)

            @pl.loop(0, (rest - odd - wides * wide) // tail)
            def _(t):
                tile(p, start, (begin + wides * wide + t * tail) * UNIT, TAIL, 0)

            @pl.when(hi > 1)
            def _():
                tile(p, start, (hi - tail) * UNIT, TAIL, UNIT)

        if which == "near":
            acc_out[p] = acc[...]
            top_out[p] = top[...]
        else:
            for h in range(QPK):
                at = slice(h * rows, (h + 1) * rows)
                result = acc[at, :DH] / acc[at, DH:]
                o_all[p, :, h * DH : (h + 1) * DH] = result.astype(jnp.bfloat16)

    if which != "near":
        for p in range(pieces):
            o_refs[p][...] = o_all[p]


def attend(dc, which, rank, doc_lengths, marks, parts, q_pieces, state=()):
    pieces = len(q_pieces)
    seq = marks.shape[0]
    held = seq // XS if which == "far" else seq
    stacked = QPK * UNIT
    vmem = pl.BlockSpec(memory_space=pltpu.VMEM)
    smem = pl.BlockSpec(memory_space=pltpu.SMEM)
    if which == "near":
        out_shape = [
            jax.ShapeDtypeStruct((pieces, stacked, 2 * DH), jnp.float32),
            jax.ShapeDtypeStruct((pieces, stacked, DH), jnp.float32),
        ]
    else:
        out_shape = [jax.ShapeDtypeStruct((UNIT, GROUP), jnp.bfloat16)] * pieces
    return pl.pallas_call(
        functools.partial(attend_kernel, pieces, dc, which),
        out_shape=out_shape,
        in_specs=[smem] * 2 + [vmem] * (1 + len(parts) + pieces + len(state)),
        out_specs=[vmem] * len(out_shape),
        scratch_shapes=[
            pltpu.VMEM((pieces, stacked, 2 * DH), jnp.bfloat16),
            pltpu.VMEM((pieces, UNIT, GROUP), jnp.bfloat16),
            pltpu.VMEM((stacked, 2 * DH), jnp.float32),
            pltpu.VMEM((stacked, DH), jnp.float32),
            pltpu.VMEM((held, DH), jnp.bfloat16),
            pltpu.VMEM((held, DH), jnp.bfloat16),
        ]
        + [pltpu.VMEM((seq, DH), jnp.bfloat16)] * (which == "near"),
        compiler_params=pltpu.CompilerParams(vmem_limit_bytes=32 * 1024 * 1024),
        cost_estimate=pl.CostEstimate(
            flops=pieces * 4 * stacked * seq // 4 * DH,
            bytes_accessed=8 * 1024 * 1024,
            transcendentals=pieces * stacked * seq // 4,
        ),
    )(rank, doc_lengths, marks, *parts, *q_pieces, *state)


def per_device(queries, keys, values, doc_lengths):
    rows = queries.shape[0]
    seq = rows * YS * XS * CS
    rank = lax.axis_index("ctx").astype(jnp.int32)
    y, x, c = place(rank)
    rank = rank[None]

    by_head = jax.ShapeDtypeStruct((KVH, 2, rows, DH), jnp.bfloat16)
    (pairs,) = vmem_call(split_kernel, [by_head], rank, keys, values)
    own = lax.all_to_all(
        pairs, "ctx", split_axis=0, concat_axis=0, tiled=True, axis_index_groups=head_groups()
    ).reshape(YS, CS, 2, rows, DH)
    doc_lengths, queries, own = lax.optimization_barrier((doc_lengths, queries, own))

    def along(part, dx):
        return lax.ppermute(part, "ctx", shift(0, dx, 0))

    left, right = along(own, 1), along(own, XS - 1)

    by_device = jax.ShapeDtypeStruct((rows, GROUP), jnp.bfloat16)
    sent = vmem_call(query_kernel, [by_device] * len(STEPS), rank, queries)
    sent = dict(zip(STEPS, sent, strict=True))

    def send(dy, dc):
        part = sent[dy, dc]
        return lax.ppermute(part, "ctx", shift(dy, 0, dc)) if dy or dc else part

    got = {(dy, 0): send(dy, 0) for dy in range(YS)}
    sent, got = lax.optimization_barrier((sent, got))
    got |= {(dy, 1): send(dy, 1) for dy in range(1, YS)}
    half = YS // 2
    far = (along(left[:half], 1), along(right[half:], XS - 1))

    doc_end = jnp.cumsum(doc_lengths)
    doc_first = doc_end - doc_lengths
    positions = jnp.arange(seq, dtype=jnp.int32)[:, None]
    inside = (doc_first[None, :] <= positions) & (positions < doc_end[None, :])
    marks = jnp.where(inside, MARK, 0.0).astype(jnp.bfloat16)
    marks = jnp.pad(marks, ((0, 0), (0, DH - marks.shape[1])))

    near = (own, left, right)
    pieces = [got[dy, 0] for dy in range(YS)]
    state = attend(0, "near", rank, doc_lengths, marks, near, pieces)
    sent, state = lax.optimization_barrier((sent, state))
    got[0, 1] = send(0, 1)
    done = attend(0, "far", rank, doc_lengths, marks, far, pieces, state)

    def give(done, dc):
        return [
            lax.ppermute(piece, "ctx", shift(YS - dy, 0, dc)) if dy or dc else piece
            for dy, piece in enumerate(done)
        ]

    done, got = lax.optimization_barrier((done, got))
    outs = give(done, 0)
    pieces = [got[dy, 1] for dy in range(YS)]
    done = attend(1, "all", rank, doc_lengths, marks, near + far, pieces)
    done, outs = lax.optimization_barrier((done, outs))
    outs += give(done, 1)

    whole = jnp.zeros((rows, H * DH), jnp.bfloat16)
    for (dy, dc), piece in zip(STEPS, outs, strict=True):
        column = group_at(y, c, dy, dc) * GROUP
        whole = lax.dynamic_update_slice(
            whole, piece, (0, column), allow_negative_indices=False
        )
    return whole


def solution(mesh):
    placed = (P(("dp", "ctx"), None), P(("dp", "ctx"), None), P(("dp", "ctx"), None), P("dp"))
    return jax.shard_map(
        per_device, mesh=mesh, in_specs=placed, out_specs=P(("dp", "ctx"), None), check_vma=False
    )
```

```python
import functools
import math

import jax
import jax.numpy as jnp
from jax import lax
from jax.experimental import pallas as pl
from jax.experimental.pallas import tpu as pltpu
from jax.sharding import PartitionSpec as P

H = 32
KVH = 8
DH = 128
QPK = H // KVH
GROUP = QPK * DH

YS = 4
XS = 4
CS = 2

UNIT = 256
TAIL = 512
WIDE = 2048
STACK = 512
MARK = 128.0
NEAR_RUN = 3
NEG_FILL = -1e30
LOG2_SCALE = math.log2(math.e) / math.sqrt(DH)


FAR = ((2, 0, YS // 2), (2, YS // 2, YS // 2))
PARTS = {"near": ((0, 0, YS), (XS - 1, 0, YS), (1, 0, YS)), "far": FAR}
PARTS["all"] = PARTS["near"] + FAR
STEPS = [(dy, dc) for dc in range(CS) for dy in range(YS)]


def ctx_index(y, x, c):
    return ((y % YS) * XS + x % XS) * CS + c % CS


def shift(dy, dx, dc):
    return [
        (ctx_index(y, x, c), ctx_index(y + dy, x + dx, c + dc))
        for y in range(YS)
        for x in range(XS)
        for c in range(CS)
    ]


def head_groups():
    return [[ctx_index(y, x, c) for y in range(YS) for c in range(CS)] for x in range(XS)]


def place(rank):
    return rank >> 3, (rank >> 1) & (XS - 1), rank & (CS - 1)


def group_at(y, c, dy, dc):
    return (((y + dy) & (YS - 1)) << 1) + (c ^ dc)


def vmem_call(kernel, out_shape, scalars, *arrays):
    smem = pl.BlockSpec(memory_space=pltpu.SMEM)
    vmem = pl.BlockSpec(memory_space=pltpu.VMEM)
    return pl.pallas_call(
        kernel,
        out_shape=out_shape,
        in_specs=[smem] * len(scalars) + [vmem] * len(arrays),
        out_specs=[vmem] * len(out_shape),
    )(*scalars, *arrays)


def split_kernel(keys, values, out):
    for h in range(KVH):
        out[h, 0] = keys[:, h * DH : (h + 1) * DH]
        out[h, 1] = values[:, h * DH : (h + 1) * DH]


def query_kernel(rank, queries, *parts):
    y, _, c = place(rank[0])
    for (dy, dc), part in zip(STEPS, parts, strict=True):
        column = pl.multiple_of(group_at(y, c, dy, dc) * GROUP, GROUP)
        part[...] = queries[:, pl.ds(column, GROUP)]


def attend_kernel(pieces, dc, which, rank, doc_lengths, marks, *refs):
    parts = PARTS[which]
    part_refs, refs = refs[: len(parts)], refs[len(parts) :]
    q_refs, refs = refs[:pieces], refs[pieces:]
    if which == "far":
        acc_in, top_in, *refs = refs
    if which == "near":
        acc_out, top_out, *refs = refs
    else:
        o_refs, refs = refs[:pieces], refs[pieces:]
    q_all, o_all, acc, top, keys, values = refs
    rows = UNIT
    y, x, c = place(rank[0])

    for (dx, first_y, ys), part in zip(parts, part_refs, strict=True):
        at_x = (x + dx) & (XS - 1)
        for i in range(ys):
            for core in range(CS):
                block = first_y + i if which == "far" else (first_y + i) * XS + at_x
                at = pl.ds(pl.multiple_of((block * CS + core) * rows, rows), rows)
                keys[at, :] = part[i, core, 0]
                values[at, :] = part[i, core, 1]
    for p in range(pieces):
        for h in range(QPK):
            q_all[p, h * rows : (h + 1) * rows, :DH] = q_refs[p][:, h * DH : (h + 1) * DH]

    def tile(p, start, first_key, size, hidden, at_row=None):
        at_key = pl.ds(pl.multiple_of(first_key if at_row is None else at_row, UNIT), size)
        if at_row is None:
            mark = marks[at_key, :]
        else:
            at_marks = [first_key + i * XS * TAIL for i in range(size // TAIL)]
            mark = [marks[pl.ds(pl.multiple_of(at, TAIL), TAIL), :] for at in at_marks]
            mark = jnp.concatenate(mark, axis=0)
        k_tile = jnp.concatenate([keys[at_key, :], mark], axis=1)
        v_tile = jnp.concatenate([values[at_key, :], jnp.ones((size, DH), jnp.bfloat16)], axis=1)
        count = QPK * rows // STACK
        stacks = [slice(i * STACK, (i + 1) * STACK) for i in range(count)]

        def multiply(i):
            return lax.dot_general(
                q_all[p, stacks[i], :],
                k_tile,
                (((1,), (1,)), ((), ())),
                preferred_element_type=jnp.float32,
            )

        def weigh(i, scores):
            if hidden:
                ahead = first_key + size - hidden - start
                q_row = lax.broadcasted_iota(jnp.int32, (STACK, hidden), 0) % rows - ahead
                keep = lax.broadcasted_iota(jnp.int32, (STACK, hidden), 1) <= q_row
                last = jnp.where(keep, scores[:, size - hidden :], NEG_FILL)
                if hidden == size:
                    scores = last
                else:
                    scores = jnp.concatenate([scores[:, : size - hidden], last], axis=1)
            old = top[stacks[i], :]
            new = jnp.maximum(old, jnp.max(scores, axis=1, keepdims=True))
            weights = jnp.exp2((scores - jnp.tile(new, (1, size // DH))) * LOG2_SCALE)
            top[stacks[i], :] = new
            return weights.astype(jnp.bfloat16), jnp.exp2((old - new) * LOG2_SCALE)

        def add(i, weights, rescale):
            acc[stacks[i], :] = acc[stacks[i], :] * jnp.tile(rescale, (1, 2)) + jnp.dot(
                weights, v_tile, preferred_element_type=jnp.float32
            )

        coming, ready = multiply(0), None
        for i in range(count):
            scores = coming
            if i + 1 < count:
                coming = multiply(i + 1)
            weighed = weigh(i, scores)
            if ready is not None:
                add(i - 1, *ready)
            ready = weighed
        add(count - 1, *ready)

    @pl.loop(0, pieces)
    def _(p):
        start = ((((y - p) & (YS - 1)) * XS + x) * CS + (c ^ dc)) * rows

        def document(d, so_far):
            first, end = so_far
            after = end + doc_lengths[d]
            return jnp.where(end <= start, end, first), after

        first, _ = lax.fori_loop(0, doc_lengths.shape[0], document, (0, 0), unroll=True)
        mark = marks[pl.ds(pl.multiple_of(start, UNIT), rows), :]
        for h in range(QPK):
            q_all[p, h * rows : (h + 1) * rows, DH:] = mark + mark

        if which == "far":
            top[...] = top_in[p]
            acc[...] = acc_in[p]

            at_x = (x + 2) & (XS - 1)
            begin = jnp.maximum(first // TAIL - at_x + XS - 1, 0) // XS
            end = jnp.maximum(start // TAIL - at_x + XS - 1, 0) // XS
            count = jnp.maximum(end - begin, 0)

            @pl.loop(0, count // 2)
            def _(t):
                key = ((begin + 2 * t) * XS + at_x) * TAIL
                tile(p, start, key, 2 * TAIL, 0, (begin + 2 * t) * TAIL)

            @pl.when(count % 2 == 1)
            def _():
                tile(p, start, ((end - 1) * XS + at_x) * TAIL, TAIL, 0, (end - 1) * TAIL)

        else:
            top[...] = jnp.full(top.shape, NEG_FILL, top.dtype)
            acc[...] = jnp.zeros(acc.shape, acc.dtype)

            lo, hi = first // UNIT, start // UNIT + 1
            tail, wide = TAIL // UNIT, WIDE // UNIT
            block = start // TAIL
            low = jnp.maximum(lo, tail * (block - 1)) if which == "near" else lo
            rest = jnp.maximum(hi - tail - low, 0)
            if which == "all":
                short = (wide - rest % wide) % wide
                rest = rest + jnp.where((short <= tail) & (short <= low), short, 0)
                low = jnp.maximum(hi - tail - rest, 0)
            odd = rest % tail
            begin = low + odd
            wides = (rest - odd) // wide
            alone = jnp.where(hi == 1, 1, odd)

            @pl.loop(0, alone)
            def _(t):
                tile(p, start, low * UNIT, UNIT, UNIT)

            if which == "all":

                @pl.loop(0, wides)
                def _(t):
                    tile(p, start, (begin + t * wide) * UNIT, WIDE, 0)

                @pl.loop(0, (rest - odd - wides * wide) // tail)
                def _(t):
                    tile(p, start, (begin + wides * wide + t * tail) * UNIT, TAIL, 0)

            else:
                @pl.loop(0, jnp.where(rest > odd, 1, 0))
                def _(t):
                    tile(p, start, begin * UNIT, TAIL, 0)

                @pl.loop(0, YS - 1)
                def _(n):
                    end = block + 2 - XS * (n + 1)
                    count = jnp.clip(end - jnp.maximum(lo // tail, 0), 0, NEAR_RUN)

                    @pl.when(count == NEAR_RUN)
                    def _():
                        tile(p, start, (end - NEAR_RUN) * TAIL, NEAR_RUN * TAIL, 0)

                    @pl.loop(0, jnp.where(count == NEAR_RUN, 0, count))
                    def _(t):
                        tile(p, start, (end - 1 - t) * TAIL, TAIL, 0)

            @pl.when(hi > 1)
            def _():
                tile(p, start, (hi - tail) * UNIT, TAIL, UNIT)

        if which == "near":
            acc_out[p] = acc[...]
            top_out[p] = top[...]
        else:
            for h in range(QPK):
                at = slice(h * rows, (h + 1) * rows)
                result = acc[at, :DH] / acc[at, DH:]
                o_all[p, :, h * DH : (h + 1) * DH] = result.astype(jnp.bfloat16)

    if which != "near":
        for p in range(pieces):
            o_refs[p][...] = o_all[p]


def attend(dc, which, rank, doc_lengths, marks, parts, q_pieces, state=()):
    pieces = len(q_pieces)
    seq = marks.shape[0]
    held = seq // XS if which == "far" else seq
    stacked = QPK * UNIT
    vmem = pl.BlockSpec(memory_space=pltpu.VMEM)
    smem = pl.BlockSpec(memory_space=pltpu.SMEM)
    if which == "near":
        out_shape = [
            jax.ShapeDtypeStruct((pieces, stacked, 2 * DH), jnp.float32),
            jax.ShapeDtypeStruct((pieces, stacked, DH), jnp.float32),
        ]
    else:
        out_shape = [jax.ShapeDtypeStruct((UNIT, GROUP), jnp.bfloat16)] * pieces
    return pl.pallas_call(
        functools.partial(attend_kernel, pieces, dc, which),
        out_shape=out_shape,
        in_specs=[smem] * 2 + [vmem] * (1 + len(parts) + pieces + len(state)),
        out_specs=[vmem] * len(out_shape),
        scratch_shapes=[
            pltpu.VMEM((pieces, stacked, 2 * DH), jnp.bfloat16),
            pltpu.VMEM((pieces, UNIT, GROUP), jnp.bfloat16),
            pltpu.VMEM((stacked, 2 * DH), jnp.float32),
            pltpu.VMEM((stacked, DH), jnp.float32),
            pltpu.VMEM((held, DH), jnp.bfloat16),
            pltpu.VMEM((held, DH), jnp.bfloat16),
        ],
        compiler_params=pltpu.CompilerParams(vmem_limit_bytes=22 * 1024 * 1024),
        cost_estimate=pl.CostEstimate(
            flops=pieces * 4 * stacked * seq // 4 * DH,
            bytes_accessed=8 * 1024 * 1024,
            transcendentals=pieces * stacked * seq // 4,
        ),
    )(rank, doc_lengths, marks, *parts, *q_pieces, *state)


def per_device(queries, keys, values, doc_lengths):
    rows = queries.shape[0]
    seq = rows * YS * XS * CS
    rank = lax.axis_index("ctx").astype(jnp.int32)
    y, x, c = place(rank)
    rank = rank[None]

    by_head = jax.ShapeDtypeStruct((KVH, 2, rows, DH), jnp.bfloat16)
    (pairs,) = vmem_call(split_kernel, [by_head], (), keys, values)
    own = lax.all_to_all(
        pairs, "ctx", split_axis=0, concat_axis=0, tiled=True, axis_index_groups=head_groups()
    ).reshape(YS, CS, 2, rows, DH)
    doc_lengths, queries, own = lax.optimization_barrier((doc_lengths, queries, own))

    def along(part, dx):
        return lax.ppermute(part, "ctx", shift(0, dx, 0))

    left, right = along(own, 1), along(own, XS - 1)

    by_device = [jax.ShapeDtypeStruct((rows, GROUP), jnp.bfloat16)] * len(STEPS)
    sent = vmem_call(query_kernel, by_device, (rank,), queries)
    sent = dict(zip(STEPS, sent, strict=True))

    def send(dy, dc):
        part = sent[dy, dc]
        return lax.ppermute(part, "ctx", shift(dy, 0, dc)) if dy or dc else part

    got = {(0, 1): send(0, 1)}
    sent, got = lax.optimization_barrier((sent, got))
    got |= {(dy, 0): send(dy, 0) for dy in range(YS)}
    sent, got = lax.optimization_barrier((sent, got))
    got |= {(dy, 1): send(dy, 1) for dy in range(1, YS)}
    half = YS // 2
    far = (along(left[:half], 1), along(right[half:], XS - 1))

    doc_end = jnp.cumsum(doc_lengths)
    doc_first = doc_end - doc_lengths
    positions = jnp.arange(seq, dtype=jnp.int32)[:, None]
    inside = (doc_first[None, :] <= positions) & (positions < doc_end[None, :])
    marks = jnp.where(inside, MARK, 0.0).astype(jnp.bfloat16)
    marks = jnp.pad(marks, ((0, 0), (0, DH - marks.shape[1])))

    near = (own, left, right)
    pieces = [got[dy, 0] for dy in range(YS)]
    state = attend(0, "near", rank, doc_lengths, marks, near, pieces)
    done = attend(0, "far", rank, doc_lengths, marks, far, pieces, state)

    def give(done, dc):
        return [
            lax.ppermute(piece, "ctx", shift(YS - dy, 0, dc)) if dy or dc else piece
            for dy, piece in enumerate(done)
        ]

    done, got = lax.optimization_barrier((done, got))
    outs = give(done, 0)
    pieces = [got[dy, 1] for dy in range(YS)]
    done = attend(1, "all", rank, doc_lengths, marks, near + far, pieces)
    done, outs = lax.optimization_barrier((done, outs))
    outs += give(done, 1)

    whole = jnp.zeros((rows, H * DH), jnp.bfloat16)
    for (dy, dc), piece in zip(STEPS, outs, strict=True):
        column = group_at(y, c, dy, dc) * GROUP
        whole = lax.dynamic_update_slice(
            whole, piece, (0, column), allow_negative_indices=False
        )
    return whole


def solution(mesh):
    placed = (P(("dp", "ctx"), None), P(("dp", "ctx"), None), P(("dp", "ctx"), None), P("dp"))
    return jax.shard_map(
        per_device, mesh=mesh, in_specs=placed, out_specs=P(("dp", "ctx"), None), check_vma=False
    )
```

```python
import functools
import math

import jax
import jax.numpy as jnp
from jax import lax
from jax.experimental import pallas as pl
from jax.experimental.pallas import tpu as pltpu
from jax.sharding import PartitionSpec as P

H = 32
KVH = 8
DH = 128
QPK = H // KVH
GROUP = QPK * DH

YS = 4
XS = 4
CS = 2

UNIT = 256
TAIL = 512
WIDE = 2048
STACK = 512
MARK = 128.0
NEAR_RUN = 3
NEG_FILL = -1e30
LOG2_SCALE = math.log2(math.e) / math.sqrt(DH)


FAR = ((2, 0, YS // 2), (2, YS // 2, YS // 2))
PARTS = {"near": ((0, 0, YS), (XS - 1, 0, YS), (1, 0, YS)), "far": FAR}
PARTS["all"] = PARTS["near"] + FAR
STEPS = [(dy, dc) for dc in range(CS) for dy in range(YS)]


def ctx_index(y, x, c):
    return ((y % YS) * XS + x % XS) * CS + c % CS


def shift(dy, dx, dc):
    return [
        (ctx_index(y, x, c), ctx_index(y + dy, x + dx, c + dc))
        for y in range(YS)
        for x in range(XS)
        for c in range(CS)
    ]


def head_groups():
    return [[ctx_index(y, x, c) for y in range(YS) for c in range(CS)] for x in range(XS)]


def place(rank):
    return rank >> 3, (rank >> 1) & (XS - 1), rank & (CS - 1)


def group_at(y, c, dy, dc):
    return (((y + dy) & (YS - 1)) << 1) + (c ^ dc)


def vmem_call(kernel, out_shape, scalars, *arrays):
    smem = pl.BlockSpec(memory_space=pltpu.SMEM)
    vmem = pl.BlockSpec(memory_space=pltpu.VMEM)
    return pl.pallas_call(
        kernel,
        out_shape=out_shape,
        in_specs=[smem] * len(scalars) + [vmem] * len(arrays),
        out_specs=[vmem] * len(out_shape),
    )(*scalars, *arrays)


def split_kernel(keys, values, out):
    for h in range(KVH):
        out[h, 0] = keys[:, h * DH : (h + 1) * DH]
        out[h, 1] = values[:, h * DH : (h + 1) * DH]


def query_kernel(rank, queries, *parts):
    y, _, c = place(rank[0])
    for (dy, dc), part in zip(STEPS, parts, strict=True):
        column = pl.multiple_of(group_at(y, c, dy, dc) * GROUP, GROUP)
        part[...] = queries[:, pl.ds(column, GROUP)]


def attend_kernel(pieces, dc, which, rank, doc_lengths, marks, *refs):
    parts = PARTS[which]
    part_refs, refs = refs[: len(parts)], refs[len(parts) :]
    q_refs, refs = refs[:pieces], refs[pieces:]
    if which == "far":
        acc_in, top_in, *refs = refs
    if which == "near":
        acc_out, top_out, *refs = refs
    else:
        o_refs, refs = refs[:pieces], refs[pieces:]
    q_all, o_all, acc, top, keys, values = refs
    rows = UNIT
    y, x, c = place(rank[0])

    for (dx, first_y, ys), part in zip(parts, part_refs, strict=True):
        at_x = (x + dx) & (XS - 1)
        for i in range(ys):
            for core in range(CS):
                block = first_y + i if which == "far" else (first_y + i) * XS + at_x
                at = pl.ds(pl.multiple_of((block * CS + core) * rows, rows), rows)
                keys[at, :] = part[i, core, 0]
                values[at, :] = part[i, core, 1]
    for p in range(pieces):
        for h in range(QPK):
            q_all[p, h * rows : (h + 1) * rows, :DH] = q_refs[p][:, h * DH : (h + 1) * DH]

    def tile(p, start, first_key, size, hidden=0, at_row=None, fresh=False):
        if which == "near":
            total, peak = acc_out.at[p], top_out.at[p]
        else:
            total, peak = acc, top
        at_key = pl.ds(pl.multiple_of(first_key if at_row is None else at_row, UNIT), size)
        if at_row is None:
            mark = marks[at_key, :]
        else:
            at_marks = [first_key + i * XS * TAIL for i in range(size // TAIL)]
            mark = [marks[pl.ds(pl.multiple_of(at, TAIL), TAIL), :] for at in at_marks]
            mark = jnp.concatenate(mark, axis=0)
        k_tile = jnp.concatenate([keys[at_key, :], mark], axis=1)
        v_tile = jnp.concatenate([values[at_key, :], jnp.ones((size, DH), jnp.bfloat16)], axis=1)
        count = QPK * rows // STACK
        stacks = [slice(i * STACK, (i + 1) * STACK) for i in range(count)]

        def multiply(i):
            return lax.dot_general(
                q_all[p, stacks[i], :],
                k_tile,
                (((1,), (1,)), ((), ())),
                preferred_element_type=jnp.float32,
            )

        def weigh(i, scores):
            if hidden:
                ahead = first_key + size - hidden - start
                q_row = lax.broadcasted_iota(jnp.int32, (STACK, hidden), 0) % rows - ahead
                keep = lax.broadcasted_iota(jnp.int32, (STACK, hidden), 1) <= q_row
                last = jnp.where(keep, scores[:, size - hidden :], NEG_FILL)
                if hidden == size:
                    scores = last
                else:
                    scores = jnp.concatenate([scores[:, : size - hidden], last], axis=1)
            new = jnp.max(scores, axis=1, keepdims=True)
            if fresh:
                new = jnp.broadcast_to(new, (STACK, DH))
            else:
                old = peak[stacks[i], :]
                new = jnp.maximum(old, new)
            weights = jnp.exp2((scores - jnp.tile(new, (1, size // DH))) * LOG2_SCALE)
            peak[stacks[i], :] = new
            rescale = None if fresh else jnp.exp2((old - new) * LOG2_SCALE)
            return weights.astype(jnp.bfloat16), rescale

        def add(i, weights, rescale):
            summed = jnp.dot(weights, v_tile, preferred_element_type=jnp.float32)
            if not fresh:
                summed = total[stacks[i], :] * jnp.tile(rescale, (1, 2)) + summed
            total[stacks[i], :] = summed

        coming, ready = multiply(0), None
        for i in range(count):
            scores = coming
            if i + 1 < count:
                coming = multiply(i + 1)
            weighed = weigh(i, scores)
            if ready is not None:
                add(i - 1, *ready)
            ready = weighed
        add(count - 1, *ready)

    @pl.loop(0, pieces)
    def _(p):
        start = ((((y - p) & (YS - 1)) * XS + x) * CS + (c ^ dc)) * rows

        def document(d, so_far):
            first, end = so_far
            after = end + doc_lengths[d]
            return jnp.where(end <= start, end, first), after

        first, _ = lax.fori_loop(0, doc_lengths.shape[0], document, (0, 0), unroll=True)
        mark = marks[pl.ds(pl.multiple_of(start, UNIT), rows), :]
        for h in range(QPK):
            q_all[p, h * rows : (h + 1) * rows, DH:] = mark + mark

        if which == "far":
            top[...] = top_in[p]
            acc[...] = acc_in[p]

            at_x = (x + 2) & (XS - 1)
            begin = jnp.maximum(first // TAIL - at_x + XS - 1, 0) // XS
            end = jnp.maximum(start // TAIL - at_x + XS - 1, 0) // XS
            count = jnp.maximum(end - begin, 0)

            @pl.loop(0, count // 2)
            def _(t):
                key = ((begin + 2 * t) * XS + at_x) * TAIL
                tile(p, start, key, 2 * TAIL, at_row=(begin + 2 * t) * TAIL)

            @pl.when(count % 2 == 1)
            def _():
                tile(p, start, ((end - 1) * XS + at_x) * TAIL, TAIL, at_row=(end - 1) * TAIL)

        else:
            lo, hi = first // UNIT, start // UNIT + 1
            tail, wide = TAIL // UNIT, WIDE // UNIT
            block = start // TAIL
            low = jnp.maximum(lo, tail * (block - 1)) if which == "near" else lo
            rest = jnp.maximum(hi - tail - low, 0)
            if which == "all":
                short = (wide - rest % wide) % wide
                rest = rest + jnp.where((short <= tail) & (short <= low), short, 0)
                low = jnp.maximum(hi - tail - rest, 0)
            odd = rest % tail
            begin = low + odd
            wides = (rest - odd) // wide

            @pl.when(hi - lo > 1)
            def _():
                tile(p, start, (hi - tail) * UNIT, TAIL, UNIT, fresh=True)

            @pl.when(hi - lo == 1)
            def _():
                tile(p, start, lo * UNIT, UNIT, UNIT, fresh=True)

            @pl.when(odd == 1)
            def _():
                tile(p, start, low * UNIT, UNIT)

            if which == "all":

                @pl.loop(0, wides)
                def _(t):
                    tile(p, start, (begin + t * wide) * UNIT, WIDE)

                @pl.loop(0, (rest - odd - wides * wide) // tail)
                def _(t):
                    tile(p, start, (begin + wides * wide + t * tail) * UNIT, TAIL)

            else:
                @pl.loop(0, jnp.where(rest > odd, 1, 0))
                def _(t):
                    tile(p, start, begin * UNIT, TAIL)

                @pl.loop(0, YS - 1)
                def _(n):
                    end = block + 2 - XS * (n + 1)
                    count = jnp.clip(end - jnp.maximum(lo // tail, 0), 0, NEAR_RUN)

                    @pl.when(count == NEAR_RUN)
                    def _():
                        tile(p, start, (end - NEAR_RUN) * TAIL, NEAR_RUN * TAIL)

                    @pl.loop(0, jnp.where(count == NEAR_RUN, 0, count))
                    def _(t):
                        tile(p, start, (end - 1 - t) * TAIL, TAIL)

        if which != "near":
            for h in range(QPK):
                at = slice(h * rows, (h + 1) * rows)
                result = acc[at, :DH] / acc[at, DH:]
                o_all[p, :, h * DH : (h + 1) * DH] = result.astype(jnp.bfloat16)

    if which != "near":
        for p in range(pieces):
            o_refs[p][...] = o_all[p]


def attend(dc, which, rank, doc_lengths, marks, parts, q_pieces, state=()):
    pieces = len(q_pieces)
    seq = marks.shape[0]
    held = seq // XS if which == "far" else seq
    stacked = QPK * UNIT
    vmem = pl.BlockSpec(memory_space=pltpu.VMEM)
    smem = pl.BlockSpec(memory_space=pltpu.SMEM)
    if which == "near":
        out_shape = [
            jax.ShapeDtypeStruct((pieces, stacked, 2 * DH), jnp.float32),
            jax.ShapeDtypeStruct((pieces, stacked, DH), jnp.float32),
        ]
    else:
        out_shape = [jax.ShapeDtypeStruct((UNIT, GROUP), jnp.bfloat16)] * pieces
    return pl.pallas_call(
        functools.partial(attend_kernel, pieces, dc, which),
        out_shape=out_shape,
        in_specs=[smem] * 2 + [vmem] * (1 + len(parts) + pieces + len(state)),
        out_specs=[vmem] * len(out_shape),
        scratch_shapes=[
            pltpu.VMEM((pieces, stacked, 2 * DH), jnp.bfloat16),
            pltpu.VMEM((pieces, UNIT, GROUP), jnp.bfloat16),
            pltpu.VMEM((stacked, 2 * DH), jnp.float32),
            pltpu.VMEM((stacked, DH), jnp.float32),
            pltpu.VMEM((held, DH), jnp.bfloat16),
            pltpu.VMEM((held, DH), jnp.bfloat16),
        ],
        compiler_params=pltpu.CompilerParams(vmem_limit_bytes=22 * 1024 * 1024),
        cost_estimate=pl.CostEstimate(
            flops=pieces * 4 * stacked * seq // 4 * DH,
            bytes_accessed=8 * 1024 * 1024,
            transcendentals=pieces * stacked * seq // 4,
        ),
    )(rank, doc_lengths, marks, *parts, *q_pieces, *state)


def per_device(queries, keys, values, doc_lengths):
    rows = queries.shape[0]
    seq = rows * YS * XS * CS
    rank = lax.axis_index("ctx").astype(jnp.int32)
    y, x, c = place(rank)
    rank = rank[None]

    by_head = jax.ShapeDtypeStruct((KVH, 2, rows, DH), jnp.bfloat16)
    (pairs,) = vmem_call(split_kernel, [by_head], (), keys, values)
    own = lax.all_to_all(
        pairs, "ctx", split_axis=0, concat_axis=0, tiled=True, axis_index_groups=head_groups()
    ).reshape(YS, CS, 2, rows, DH)
    doc_lengths, queries, own = lax.optimization_barrier((doc_lengths, queries, own))

    def along(part, dx):
        return lax.ppermute(part, "ctx", shift(0, dx, 0))

    left, right = along(own, 1), along(own, XS - 1)

    by_device = [jax.ShapeDtypeStruct((rows, GROUP), jnp.bfloat16)] * len(STEPS)
    sent = vmem_call(query_kernel, by_device, (rank,), queries)
    sent = dict(zip(STEPS, sent, strict=True))

    def send(dy, dc):
        part = sent[dy, dc]
        return lax.ppermute(part, "ctx", shift(dy, 0, dc)) if dy or dc else part

    got = {(0, 1): send(0, 1)}
    sent, got = lax.optimization_barrier((sent, got))
    got |= {(dy, 0): send(dy, 0) for dy in range(YS)}
    sent, got = lax.optimization_barrier((sent, got))
    got |= {(dy, 1): send(dy, 1) for dy in range(1, YS)}
    half = YS // 2
    far = (along(left[:half], 1), along(right[half:], XS - 1))

    doc_end = jnp.cumsum(doc_lengths)
    doc_first = doc_end - doc_lengths
    positions = jnp.arange(seq, dtype=jnp.int32)[:, None]
    inside = (doc_first[None, :] <= positions) & (positions < doc_end[None, :])
    marks = jnp.where(inside, MARK, 0.0).astype(jnp.bfloat16)
    marks = jnp.pad(marks, ((0, 0), (0, DH - marks.shape[1])))

    near = (own, left, right)
    pieces = [got[dy, 0] for dy in range(YS)]
    state = attend(0, "near", rank, doc_lengths, marks, near, pieces)
    done = attend(0, "far", rank, doc_lengths, marks, far, pieces, state)

    def give(done, dc):
        return [
            lax.ppermute(piece, "ctx", shift(YS - dy, 0, dc)) if dy or dc else piece
            for dy, piece in enumerate(done)
        ]

    done, got = lax.optimization_barrier((done, got))
    outs = give(done, 0)
    pieces = [got[dy, 1] for dy in range(YS)]
    done = attend(1, "all", rank, doc_lengths, marks, near + far, pieces)
    done, outs = lax.optimization_barrier((done, outs))
    outs += give(done, 1)

    whole = jnp.zeros((rows, H * DH), jnp.bfloat16)
    for (dy, dc), piece in zip(STEPS, outs, strict=True):
        column = group_at(y, c, dy, dc) * GROUP
        whole = lax.dynamic_update_slice(
            whole, piece, (0, column), allow_negative_indices=False
        )
    return whole


def solution(mesh):
    placed = (P(("dp", "ctx"), None), P(("dp", "ctx"), None), P(("dp", "ctx"), None), P("dp"))
    return jax.shard_map(
        per_device, mesh=mesh, in_specs=placed, out_specs=P(("dp", "ctx"), None), check_vma=False
    )
```

```python
import functools
import math

import jax
import jax.numpy as jnp
from jax import lax
from jax.experimental import pallas as pl
from jax.experimental.pallas import tpu as pltpu
from jax.sharding import PartitionSpec as P

H = 32
KVH = 8
DH = 128
QPK = H // KVH
GROUP = QPK * DH

YS = 4
XS = 4
CS = 2

UNIT = 256
TAIL = 512
WIDE = 2048
STACK = 512
MARK = 128.0
NEAR_RUN = 3
NEG_FILL = -1e30
LOG2_SCALE = math.log2(math.e) / math.sqrt(DH)


FAR = ((2, 0, YS // 2), (2, YS // 2, YS // 2))
PARTS = {"near": ((0, 0, YS), (XS - 1, 0, YS), (1, 0, YS)), "far": FAR}
PARTS["all"] = PARTS["near"] + FAR
STEPS = [(dy, int(dy == 0) ^ half) for half in range(CS) for dy in range(YS)]


def ctx_index(y, x, c):
    return ((y % YS) * XS + x % XS) * CS + c % CS


def shift(dy, dx, dc):
    return [
        (ctx_index(y, x, c), ctx_index(y + dy, x + dx, c + dc))
        for y in range(YS)
        for x in range(XS)
        for c in range(CS)
    ]


def head_groups():
    return [[ctx_index(y, x, c) for y in range(YS) for c in range(CS)] for x in range(XS)]


def place(rank):
    return rank >> 3, (rank >> 1) & (XS - 1), rank & (CS - 1)


def group_at(y, c, dy, dc):
    return (((y + dy) & (YS - 1)) << 1) + (c ^ dc)


def vmem_call(kernel, out_shape, scalars, *arrays):
    smem = pl.BlockSpec(memory_space=pltpu.SMEM)
    vmem = pl.BlockSpec(memory_space=pltpu.VMEM)
    return pl.pallas_call(
        kernel,
        out_shape=out_shape,
        in_specs=[smem] * len(scalars) + [vmem] * len(arrays),
        out_specs=[vmem] * len(out_shape),
    )(*scalars, *arrays)


def split_kernel(keys, values, out):
    for h in range(KVH):
        out[h, 0] = keys[:, h * DH : (h + 1) * DH]
        out[h, 1] = values[:, h * DH : (h + 1) * DH]


def query_kernel(rank, queries, *parts):
    y, _, c = place(rank[0])
    for (dy, dc), part in zip(STEPS, parts, strict=True):
        column = pl.multiple_of(group_at(y, c, dy, dc) * GROUP, GROUP)
        part[...] = queries[:, pl.ds(column, GROUP)]


def attend_kernel(pieces, half, which, rank, doc_lengths, marks, *refs):
    parts = PARTS[which]
    part_refs, refs = refs[: len(parts)], refs[len(parts) :]
    q_refs, refs = refs[:pieces], refs[pieces:]
    if which == "far":
        acc_in, top_in, *refs = refs
    if which == "near":
        acc_out, top_out, *refs = refs
    else:
        o_refs, refs = refs[:pieces], refs[pieces:]
    q_all, o_all, acc, top, keys, values = refs
    rows = UNIT
    y, x, c = place(rank[0])

    for (dx, first_y, ys), part in zip(parts, part_refs, strict=True):
        at_x = (x + dx) & (XS - 1)
        for i in range(ys):
            for core in range(CS):
                block = first_y + i if which == "far" else (first_y + i) * XS + at_x
                at = pl.ds(pl.multiple_of((block * CS + core) * rows, rows), rows)
                keys[at, :] = part[i, core, 0]
                values[at, :] = part[i, core, 1]
    for p in range(pieces):
        for h in range(QPK):
            q_all[p, h * rows : (h + 1) * rows, :DH] = q_refs[p][:, h * DH : (h + 1) * DH]

    def tile(p, start, first_key, size, hidden=0, at_row=None, fresh=False):
        if which == "near":
            total, peak = acc_out.at[p], top_out.at[p]
        else:
            total, peak = acc, top
        at_key = pl.ds(pl.multiple_of(first_key if at_row is None else at_row, UNIT), size)
        if at_row is None:
            mark = marks[at_key, :]
        else:
            at_marks = [first_key + i * XS * TAIL for i in range(size // TAIL)]
            mark = [marks[pl.ds(pl.multiple_of(at, TAIL), TAIL), :] for at in at_marks]
            mark = jnp.concatenate(mark, axis=0)
        k_tile = jnp.concatenate([keys[at_key, :], mark], axis=1)
        v_tile = jnp.concatenate([values[at_key, :], jnp.ones((size, DH), jnp.bfloat16)], axis=1)
        count = QPK * rows // STACK
        stacks = [slice(i * STACK, (i + 1) * STACK) for i in range(count)]

        def multiply(i):
            return lax.dot_general(
                q_all[p, stacks[i], :],
                k_tile,
                (((1,), (1,)), ((), ())),
                preferred_element_type=jnp.float32,
            )

        def weigh(i, scores):
            if hidden:
                ahead = first_key + size - hidden - start
                q_row = lax.broadcasted_iota(jnp.int32, (STACK, hidden), 0) % rows - ahead
                keep = lax.broadcasted_iota(jnp.int32, (STACK, hidden), 1) <= q_row
                last = jnp.where(keep, scores[:, size - hidden :], NEG_FILL)
                if hidden == size:
                    scores = last
                else:
                    scores = jnp.concatenate([scores[:, : size - hidden], last], axis=1)
            new = jnp.max(scores, axis=1, keepdims=True)
            if fresh:
                new = jnp.broadcast_to(new, (STACK, DH))
            else:
                old = peak[stacks[i], :]
                new = jnp.maximum(old, new)
            weights = jnp.exp2((scores - jnp.tile(new, (1, size // DH))) * LOG2_SCALE)
            peak[stacks[i], :] = new
            rescale = None if fresh else jnp.exp2((old - new) * LOG2_SCALE)
            return weights.astype(jnp.bfloat16), rescale

        def add(i, weights, rescale):
            summed = jnp.dot(weights, v_tile, preferred_element_type=jnp.float32)
            if not fresh:
                summed = total[stacks[i], :] * jnp.tile(rescale, (1, 2)) + summed
            total[stacks[i], :] = summed

        coming, ready = multiply(0), None
        for i in range(count):
            scores = coming
            if i + 1 < count:
                coming = multiply(i + 1)
            weighed = weigh(i, scores)
            if ready is not None:
                add(i - 1, *ready)
            ready = weighed
        add(count - 1, *ready)

    @pl.loop(0, pieces)
    def _(p):
        dc = jnp.where(p == 0, 1 - half, half)
        start = ((((y - p) & (YS - 1)) * XS + x) * CS + (c ^ dc)) * rows

        def document(d, so_far):
            first, end = so_far
            after = end + doc_lengths[d]
            return jnp.where(end <= start, end, first), after

        first, _ = lax.fori_loop(0, doc_lengths.shape[0], document, (0, 0), unroll=True)
        mark = marks[pl.ds(pl.multiple_of(start, UNIT), rows), :]
        for h in range(QPK):
            q_all[p, h * rows : (h + 1) * rows, DH:] = mark + mark

        if which == "far":
            top[...] = top_in[p]
            acc[...] = acc_in[p]

            at_x = (x + 2) & (XS - 1)
            begin = jnp.maximum(first // TAIL - at_x + XS - 1, 0) // XS
            end = jnp.maximum(start // TAIL - at_x + XS - 1, 0) // XS
            count = jnp.maximum(end - begin, 0)

            @pl.loop(0, count // 2)
            def _(t):
                key = ((begin + 2 * t) * XS + at_x) * TAIL
                tile(p, start, key, 2 * TAIL, at_row=(begin + 2 * t) * TAIL)

            @pl.when(count % 2 == 1)
            def _():
                tile(p, start, ((end - 1) * XS + at_x) * TAIL, TAIL, at_row=(end - 1) * TAIL)

        else:
            lo, hi = first // UNIT, start // UNIT + 1
            tail, wide = TAIL // UNIT, WIDE // UNIT
            block = start // TAIL
            low = jnp.maximum(lo, tail * (block - 1)) if which == "near" else lo
            rest = jnp.maximum(hi - tail - low, 0)
            if which == "all":
                short = (wide - rest % wide) % wide
                rest = rest + jnp.where((short <= tail) & (short <= low), short, 0)
                low = jnp.maximum(hi - tail - rest, 0)
            odd = rest % tail
            begin = low + odd
            wides = (rest - odd) // wide

            @pl.when(hi - lo > 1)
            def _():
                tile(p, start, (hi - tail) * UNIT, TAIL, UNIT, fresh=True)

            @pl.when(hi - lo == 1)
            def _():
                tile(p, start, lo * UNIT, UNIT, UNIT, fresh=True)

            @pl.when(odd == 1)
            def _():
                tile(p, start, low * UNIT, UNIT)

            if which == "all":

                @pl.loop(0, wides)
                def _(t):
                    tile(p, start, (begin + t * wide) * UNIT, WIDE)

                @pl.loop(0, (rest - odd - wides * wide) // tail)
                def _(t):
                    tile(p, start, (begin + wides * wide + t * tail) * UNIT, TAIL)

            else:
                @pl.loop(0, jnp.where(rest > odd, 1, 0))
                def _(t):
                    tile(p, start, begin * UNIT, TAIL)

                @pl.loop(0, YS - 1)
                def _(n):
                    end = block + 2 - XS * (n + 1)
                    count = jnp.clip(end - jnp.maximum(lo // tail, 0), 0, NEAR_RUN)

                    @pl.when(count == NEAR_RUN)
                    def _():
                        tile(p, start, (end - NEAR_RUN) * TAIL, NEAR_RUN * TAIL)

                    @pl.loop(0, jnp.where(count == NEAR_RUN, 0, count))
                    def _(t):
                        tile(p, start, (end - 1 - t) * TAIL, TAIL)

        if which != "near":
            for h in range(QPK):
                at = slice(h * rows, (h + 1) * rows)
                result = acc[at, :DH] / acc[at, DH:]
                o_all[p, :, h * DH : (h + 1) * DH] = result.astype(jnp.bfloat16)

    if which != "near":
        for p in range(pieces):
            o_refs[p][...] = o_all[p]


def attend(half, which, rank, doc_lengths, marks, parts, q_pieces, state=()):
    pieces = len(q_pieces)
    seq = marks.shape[0]
    held = seq // XS if which == "far" else seq
    stacked = QPK * UNIT
    vmem = pl.BlockSpec(memory_space=pltpu.VMEM)
    smem = pl.BlockSpec(memory_space=pltpu.SMEM)
    if which == "near":
        out_shape = [
            jax.ShapeDtypeStruct((pieces, stacked, 2 * DH), jnp.float32),
            jax.ShapeDtypeStruct((pieces, stacked, DH), jnp.float32),
        ]
    else:
        out_shape = [jax.ShapeDtypeStruct((UNIT, GROUP), jnp.bfloat16)] * pieces
    return pl.pallas_call(
        functools.partial(attend_kernel, pieces, half, which),
        out_shape=out_shape,
        in_specs=[smem] * 2 + [vmem] * (1 + len(parts) + pieces + len(state)),
        out_specs=[vmem] * len(out_shape),
        scratch_shapes=[
            pltpu.VMEM((pieces, stacked, 2 * DH), jnp.bfloat16),
            pltpu.VMEM((pieces, UNIT, GROUP), jnp.bfloat16),
            pltpu.VMEM((stacked, 2 * DH), jnp.float32),
            pltpu.VMEM((stacked, DH), jnp.float32),
            pltpu.VMEM((held, DH), jnp.bfloat16),
            pltpu.VMEM((held, DH), jnp.bfloat16),
        ],
        compiler_params=pltpu.CompilerParams(vmem_limit_bytes=22 * 1024 * 1024),
        cost_estimate=pl.CostEstimate(
            flops=pieces * 4 * stacked * seq // 4 * DH,
            bytes_accessed=8 * 1024 * 1024,
            transcendentals=pieces * stacked * seq // 4,
        ),
    )(rank, doc_lengths, marks, *parts, *q_pieces, *state)


def per_device(queries, keys, values, doc_lengths):
    rows = queries.shape[0]
    seq = rows * YS * XS * CS
    rank = lax.axis_index("ctx").astype(jnp.int32)
    y, x, c = place(rank)
    rank = rank[None]

    by_head = jax.ShapeDtypeStruct((KVH, 2, rows, DH), jnp.bfloat16)
    (pairs,) = vmem_call(split_kernel, [by_head], (), keys, values)
    own = lax.all_to_all(
        pairs, "ctx", split_axis=0, concat_axis=0, tiled=True, axis_index_groups=head_groups()
    ).reshape(YS, CS, 2, rows, DH)
    doc_lengths, queries, own = lax.optimization_barrier((doc_lengths, queries, own))

    def along(part, dx):
        return lax.ppermute(part, "ctx", shift(0, dx, 0))

    left, right = along(own, 1), along(own, XS - 1)

    by_device = [jax.ShapeDtypeStruct((rows, GROUP), jnp.bfloat16)] * len(STEPS)
    sent = vmem_call(query_kernel, by_device, (rank,), queries)
    sent = dict(zip(STEPS, sent, strict=True))

    def send(dy, dc):
        part = sent[dy, dc]
        return lax.ppermute(part, "ctx", shift(dy, 0, dc)) if dy or dc else part

    first_half, second_half = STEPS[:YS], STEPS[YS:]
    got = {(0, 1): send(0, 1)}
    sent, got = lax.optimization_barrier((sent, got))
    got |= {step: send(*step) for step in first_half if step not in got}
    sent, got = lax.optimization_barrier((sent, got))
    got |= {step: send(*step) for step in second_half}
    some = YS // 2
    far = (along(left[:some], 1), along(right[some:], XS - 1))

    doc_end = jnp.cumsum(doc_lengths)
    doc_first = doc_end - doc_lengths
    positions = jnp.arange(seq, dtype=jnp.int32)[:, None]
    inside = (doc_first[None, :] <= positions) & (positions < doc_end[None, :])
    marks = jnp.where(inside, MARK, 0.0).astype(jnp.bfloat16)
    marks = jnp.pad(marks, ((0, 0), (0, DH - marks.shape[1])))

    near = (own, left, right)
    pieces = [got[step] for step in first_half]
    state = attend(0, "near", rank, doc_lengths, marks, near, pieces)
    done = attend(0, "far", rank, doc_lengths, marks, far, pieces, state)

    def give(done, steps):
        return [
            lax.ppermute(piece, "ctx", shift(YS - dy, 0, dc)) if dy or dc else piece
            for (dy, dc), piece in zip(steps, done, strict=True)
        ]

    done, got = lax.optimization_barrier((done, got))
    outs = give(done, first_half)
    pieces = [got[step] for step in second_half]
    done = attend(1, "all", rank, doc_lengths, marks, near + far, pieces)
    in_chip, *across = outs
    done, across = lax.optimization_barrier((done, across))
    outs = [in_chip, *across, *give(done, second_half)]

    whole = jnp.zeros((rows, H * DH), jnp.bfloat16)
    for (dy, dc), piece in zip(STEPS, outs, strict=True):
        column = group_at(y, c, dy, dc) * GROUP
        whole = lax.dynamic_update_slice(
            whole, piece, (0, column), allow_negative_indices=False
        )
    return whole


def solution(mesh):
    placed = (P(("dp", "ctx"), None), P(("dp", "ctx"), None), P(("dp", "ctx"), None), P("dp"))
    return jax.shard_map(
        per_device, mesh=mesh, in_specs=placed, out_specs=P(("dp", "ctx"), None), check_vma=False
    )
```

```python
import functools
import math

import jax
import jax.numpy as jnp
from jax import lax
from jax.experimental import pallas as pl
from jax.experimental.pallas import tpu as pltpu
from jax.sharding import PartitionSpec as P

H = 32
KVH = 8
DH = 128
QPK = H // KVH
GROUP = QPK * DH

YS = 4
XS = 4
CS = 2

UNIT = 256
TAIL = 512
WIDE = 2048
STACK = 512
MARK = 128.0
NEAR_RUN = 3
NEG_FILL = -1e30
LOG2_SCALE = math.log2(math.e) / math.sqrt(DH)


FAR = ((2, 0, YS // 2), (2, YS // 2, YS // 2))
PARTS = {"near": ((0, 0, YS), (XS - 1, 0, YS), (1, 0, YS)), "far": FAR}
PARTS["all"] = PARTS["near"] + FAR
STEPS = [(dy, int(dy == 0) ^ half) for half in range(CS) for dy in range(YS)]


def ctx_index(y, x, c):
    return ((y % YS) * XS + x % XS) * CS + c % CS


def shift(dy, dx, dc):
    return [
        (ctx_index(y, x, c), ctx_index(y + dy, x + dx, c + dc))
        for y in range(YS)
        for x in range(XS)
        for c in range(CS)
    ]


def head_groups():
    return [[ctx_index(y, x, c) for y in range(YS) for c in range(CS)] for x in range(XS)]


def place(rank):
    return rank >> 3, (rank >> 1) & (XS - 1), rank & (CS - 1)


def group_at(y, c, dy, dc):
    return (((y + dy) & (YS - 1)) << 1) + (c ^ dc)


def vmem_call(kernel, out_shape, scalars, *arrays):
    smem = pl.BlockSpec(memory_space=pltpu.SMEM)
    vmem = pl.BlockSpec(memory_space=pltpu.VMEM)
    return pl.pallas_call(
        kernel,
        out_shape=out_shape,
        in_specs=[smem] * len(scalars) + [vmem] * len(arrays),
        out_specs=[vmem] * len(out_shape),
    )(*scalars, *arrays)


def split_kernel(keys, values, out):
    for h in range(KVH):
        out[h, 0] = keys[:, h * DH : (h + 1) * DH]
        out[h, 1] = values[:, h * DH : (h + 1) * DH]


def query_kernel(rank, queries, *parts):
    y, _, c = place(rank[0])
    for (dy, dc), part in zip(STEPS, parts, strict=True):
        column = pl.multiple_of(group_at(y, c, dy, dc) * GROUP, GROUP)
        part[...] = queries[:, pl.ds(column, GROUP)]


def attend_kernel(pieces, half, which, rank, doc_lengths, marks, *refs):
    parts = PARTS[which]
    part_refs, refs = refs[: len(parts)], refs[len(parts) :]
    q_refs, refs = refs[:pieces], refs[pieces:]
    if which == "far":
        acc_in, top_in, *refs = refs
    if which == "near":
        acc_out, top_out, *refs = refs
    else:
        o_refs, refs = refs[:pieces], refs[pieces:]
    q_all, o_all, acc, top, keys, values = refs
    rows = UNIT
    y, x, c = place(rank[0])

    for (dx, first_y, ys), part in zip(parts, part_refs, strict=True):
        at_x = (x + dx) & (XS - 1)
        for i in range(ys):
            for core in range(CS):
                block = first_y + i if which == "far" else (first_y + i) * XS + at_x
                at = pl.ds(pl.multiple_of((block * CS + core) * rows, rows), rows)
                keys[at, :] = part[i, core, 0]
                values[at, :] = part[i, core, 1]
    for p in range(pieces):
        for h in range(QPK):
            q_all[p, h * rows : (h + 1) * rows, :DH] = q_refs[p][:, h * DH : (h + 1) * DH]

    def tile(p, start, first_key, size, hidden=0, at_row=None, fresh=False):
        if which == "near":
            total, peak = acc_out.at[p], top_out.at[p]
        else:
            total, peak = acc, top
        at_key = pl.ds(pl.multiple_of(first_key if at_row is None else at_row, UNIT), size)
        if at_row is None:
            mark = marks[at_key, :]
        else:
            at_marks = [first_key + i * XS * TAIL for i in range(size // TAIL)]
            mark = [marks[pl.ds(pl.multiple_of(at, TAIL), TAIL), :] for at in at_marks]
            mark = jnp.concatenate(mark, axis=0)
        k_tile = jnp.concatenate([keys[at_key, :], mark], axis=1)
        v_tile = jnp.concatenate([values[at_key, :], jnp.ones((size, DH), jnp.bfloat16)], axis=1)
        count = QPK * rows // STACK
        stacks = [slice(i * STACK, (i + 1) * STACK) for i in range(count)]

        def multiply(i):
            return lax.dot_general(
                q_all[p, stacks[i], :],
                k_tile,
                (((1,), (1,)), ((), ())),
                preferred_element_type=jnp.float32,
            )

        def weigh(i, scores):
            if hidden:
                ahead = first_key + size - hidden - start
                q_row = lax.broadcasted_iota(jnp.int32, (STACK, hidden), 0) % rows - ahead
                keep = lax.broadcasted_iota(jnp.int32, (STACK, hidden), 1) <= q_row
                last = jnp.where(keep, scores[:, size - hidden :], NEG_FILL)
                if hidden == size:
                    scores = last
                else:
                    scores = jnp.concatenate([scores[:, : size - hidden], last], axis=1)
            new = jnp.max(scores, axis=1, keepdims=True)
            if fresh:
                new = jnp.broadcast_to(new, (STACK, DH))
            else:
                old = peak[stacks[i], :]
                new = jnp.maximum(old, new)
            weights = jnp.exp2((scores - jnp.tile(new, (1, size // DH))) * LOG2_SCALE)
            peak[stacks[i], :] = new
            rescale = None if fresh else jnp.exp2((old - new) * LOG2_SCALE)
            return weights.astype(jnp.bfloat16), rescale

        def add(i, weights, rescale):
            summed = jnp.dot(weights, v_tile, preferred_element_type=jnp.float32)
            if not fresh:
                summed = total[stacks[i], :] * jnp.tile(rescale, (1, 2)) + summed
            total[stacks[i], :] = summed

        coming, ready = multiply(0), None
        for i in range(count):
            scores = coming
            if i + 1 < count:
                coming = multiply(i + 1)
            weighed = weigh(i, scores)
            if ready is not None:
                add(i - 1, *ready)
            ready = weighed
        add(count - 1, *ready)

    @pl.loop(0, pieces)
    def _(p):
        dc = jnp.where(p == 0, 1 - half, half)
        start = ((((y - p) & (YS - 1)) * XS + x) * CS + (c ^ dc)) * rows

        def document(d, so_far):
            first, end = so_far
            after = end + doc_lengths[d]
            return jnp.where(end <= start, end, first), after

        first, _ = lax.fori_loop(0, doc_lengths.shape[0], document, (0, 0), unroll=True)
        mark = marks[pl.ds(pl.multiple_of(start, UNIT), rows), :]
        for h in range(QPK):
            q_all[p, h * rows : (h + 1) * rows, DH:] = mark + mark

        if which == "far":
            top[...] = top_in[p]
            acc[...] = acc_in[p]

            at_x = (x + 2) & (XS - 1)
            begin = jnp.maximum(first // TAIL - at_x + XS - 1, 0) // XS
            end = jnp.maximum(start // TAIL - at_x + XS - 1, 0) // XS
            count = jnp.maximum(end - begin, 0)

            @pl.loop(0, count // 2)
            def _(t):
                key = ((begin + 2 * t) * XS + at_x) * TAIL
                tile(p, start, key, 2 * TAIL, at_row=(begin + 2 * t) * TAIL)

            @pl.when(count % 2 == 1)
            def _():
                tile(p, start, ((end - 1) * XS + at_x) * TAIL, TAIL, at_row=(end - 1) * TAIL)

        else:
            lo, hi = first // UNIT, start // UNIT + 1
            tail, wide = TAIL // UNIT, WIDE // UNIT
            block = start // TAIL
            low = jnp.maximum(lo, tail * (block - 1)) if which == "near" else lo
            rest = jnp.maximum(hi - tail - low, 0)
            if which == "all":
                short = (wide - rest % wide) % wide
                rest = rest + jnp.where((short <= tail) & (short <= low), short, 0)
                low = jnp.maximum(hi - tail - rest, 0)
            odd = rest % tail
            begin = low + odd
            wides = (rest - odd) // wide

            @pl.when(hi - lo > 1)
            def _():
                tile(p, start, (hi - tail) * UNIT, TAIL, UNIT, fresh=True)

            @pl.when(hi - lo == 1)
            def _():
                tile(p, start, lo * UNIT, UNIT, UNIT, fresh=True)

            @pl.when(odd == 1)
            def _():
                tile(p, start, low * UNIT, UNIT)

            if which == "all":

                @pl.loop(0, wides)
                def _(t):
                    tile(p, start, (begin + t * wide) * UNIT, WIDE)

                @pl.loop(0, (rest - odd - wides * wide) // tail)
                def _(t):
                    tile(p, start, (begin + wides * wide + t * tail) * UNIT, TAIL)

            else:
                @pl.loop(0, jnp.where(rest > odd, 1, 0))
                def _(t):
                    tile(p, start, begin * UNIT, TAIL)

                @pl.loop(0, YS - 1)
                def _(n):
                    end = block + 2 - XS * (n + 1)
                    count = jnp.clip(end - jnp.maximum(lo // tail, 0), 0, NEAR_RUN)

                    @pl.when(count == NEAR_RUN)
                    def _():
                        tile(p, start, (end - NEAR_RUN) * TAIL, NEAR_RUN * TAIL)

                    @pl.loop(0, jnp.where(count == NEAR_RUN, 0, count))
                    def _(t):
                        tile(p, start, (end - 1 - t) * TAIL, TAIL)

        if which != "near":
            for h in range(QPK):
                at = slice(h * rows, (h + 1) * rows)
                result = acc[at, :DH] / acc[at, DH:]
                o_all[p, :, h * DH : (h + 1) * DH] = result.astype(jnp.bfloat16)

    if which != "near":
        for p in range(pieces):
            o_refs[p][...] = o_all[p]


def attend(half, which, rank, doc_lengths, marks, parts, q_pieces, state=()):
    pieces = len(q_pieces)
    seq = marks.shape[0]
    held = seq // XS if which == "far" else seq
    stacked = QPK * UNIT
    vmem = pl.BlockSpec(memory_space=pltpu.VMEM)
    smem = pl.BlockSpec(memory_space=pltpu.SMEM)
    if which == "near":
        out_shape = [
            jax.ShapeDtypeStruct((pieces, stacked, 2 * DH), jnp.float32),
            jax.ShapeDtypeStruct((pieces, stacked, DH), jnp.float32),
        ]
    else:
        out_shape = [jax.ShapeDtypeStruct((UNIT, GROUP), jnp.bfloat16)] * pieces
    return pl.pallas_call(
        functools.partial(attend_kernel, pieces, half, which),
        out_shape=out_shape,
        in_specs=[smem] * 2 + [vmem] * (1 + len(parts) + pieces + len(state)),
        out_specs=[vmem] * len(out_shape),
        scratch_shapes=[
            pltpu.VMEM((pieces, stacked, 2 * DH), jnp.bfloat16),
            pltpu.VMEM((pieces, UNIT, GROUP), jnp.bfloat16),
            pltpu.VMEM((stacked, 2 * DH), jnp.float32),
            pltpu.VMEM((stacked, DH), jnp.float32),
            pltpu.VMEM((held, DH), jnp.bfloat16),
            pltpu.VMEM((held, DH), jnp.bfloat16),
        ],
        compiler_params=pltpu.CompilerParams(vmem_limit_bytes=22 * 1024 * 1024),
        cost_estimate=pl.CostEstimate(
            flops=pieces * 4 * stacked * seq // 4 * DH,
            bytes_accessed=8 * 1024 * 1024,
            transcendentals=pieces * stacked * seq // 4,
        ),
    )(rank, doc_lengths, marks, *parts, *q_pieces, *state)


def per_device(queries, keys, values, doc_lengths):
    rows = queries.shape[0]
    seq = rows * YS * XS * CS
    rank = lax.axis_index("ctx").astype(jnp.int32)
    y, x, c = place(rank)
    rank = rank[None]

    by_head = jax.ShapeDtypeStruct((KVH, 2, rows, DH), jnp.bfloat16)
    (pairs,) = vmem_call(split_kernel, [by_head], (), keys, values)
    own = lax.all_to_all(
        pairs, "ctx", split_axis=0, concat_axis=0, tiled=True, axis_index_groups=head_groups()
    ).reshape(YS, CS, 2, rows, DH)
    doc_lengths, queries, own = lax.optimization_barrier((doc_lengths, queries, own))

    def along(part, dx):
        return lax.ppermute(part, "ctx", shift(0, dx, 0))

    left, right = along(own, 1), along(own, XS - 1)

    by_device = [jax.ShapeDtypeStruct((rows, GROUP), jnp.bfloat16)] * len(STEPS)
    sent = vmem_call(query_kernel, by_device, (rank,), queries)
    sent = dict(zip(STEPS, sent, strict=True))

    def send(dy, dc):
        part = sent[dy, dc]
        return lax.ppermute(part, "ctx", shift(dy, 0, dc)) if dy or dc else part

    first_half, second_half = STEPS[:YS], STEPS[YS:]
    got = {(0, 1): send(0, 1)}
    sent, got = lax.optimization_barrier((sent, got))
    got |= {step: send(*step) for step in first_half if step not in got}
    sent, got = lax.optimization_barrier((sent, got))
    got |= {step: send(*step) for step in second_half}
    some = YS // 2
    far = (along(left[:some], 1), along(right[some:], XS - 1))

    doc_end = jnp.cumsum(doc_lengths)
    none = jnp.zeros((DH - doc_end.shape[0],), jnp.int32)
    doc_first = jnp.concatenate([doc_end - doc_lengths, none])
    doc_end = jnp.concatenate([doc_end, none])
    positions = jnp.arange(seq, dtype=jnp.int32)[:, None]
    inside = (doc_first[None, :] <= positions) & (positions < doc_end[None, :])
    marks = jnp.where(inside, MARK, 0.0).astype(jnp.bfloat16)

    near = (own, left, right)
    pieces = [got[step] for step in first_half]
    state = attend(0, "near", rank, doc_lengths, marks, near, pieces)
    done = attend(0, "far", rank, doc_lengths, marks, far, pieces, state)

    def give(done, steps):
        return [
            lax.ppermute(piece, "ctx", shift(YS - dy, 0, dc)) if dy or dc else piece
            for (dy, dc), piece in zip(steps, done, strict=True)
        ]

    done, got = lax.optimization_barrier((done, got))
    outs = give(done, first_half)
    pieces = [got[step] for step in second_half]
    done = attend(1, "all", rank, doc_lengths, marks, near + far, pieces)
    in_chip, *across = outs
    done, across = lax.optimization_barrier((done, across))
    outs = [in_chip, *across, *give(done, second_half)]

    whole = jnp.zeros((rows, H * DH), jnp.bfloat16)
    for (dy, dc), piece in zip(STEPS, outs, strict=True):
        column = group_at(y, c, dy, dc) * GROUP
        whole = lax.dynamic_update_slice(
            whole, piece, (0, column), allow_negative_indices=False
        )
    return whole


def solution(mesh):
    placed = (P(("dp", "ctx"), None), P(("dp", "ctx"), None), P(("dp", "ctx"), None), P("dp"))
    return jax.shard_map(
        per_device, mesh=mesh, in_specs=placed, out_specs=P(("dp", "ctx"), None), check_vma=False
    )
```

```python
import functools
import math

import jax
import jax.numpy as jnp
from jax import lax
from jax.experimental import pallas as pl
from jax.experimental.pallas import tpu as pltpu
from jax.sharding import PartitionSpec as P

H = 32
KVH = 8
DH = 128
QPK = H // KVH
GROUP = QPK * DH

YS = 4
XS = 4
CS = 2

UNIT = 256
TAIL = 512
WIDE = 2048
STACK = 512
MARK = 128.0
NEAR_RUN = 3
NEG_FILL = -1e30
LOG2_SCALE = math.log2(math.e) / math.sqrt(DH)


FAR = ((2, 0, YS // 2), (2, YS // 2, YS // 2))
PARTS = {"near": ((0, 0, YS), (XS - 1, 0, YS), (1, 0, YS)), "far": FAR}
PARTS["all"] = PARTS["near"] + FAR
STEPS = [(dy, int(dy == 0) ^ half) for half in range(CS) for dy in range(YS)]


def ctx_index(y, x, c):
    return ((y % YS) * XS + x % XS) * CS + c % CS


def shift(dy, dx, dc):
    return [
        (ctx_index(y, x, c), ctx_index(y + dy, x + dx, c + dc))
        for y in range(YS)
        for x in range(XS)
        for c in range(CS)
    ]


def head_groups():
    return [[ctx_index(y, x, c) for y in range(YS) for c in range(CS)] for x in range(XS)]


def place(rank):
    return rank >> 3, (rank >> 1) & (XS - 1), rank & (CS - 1)


def group_at(y, c, dy, dc):
    return (((y + dy) & (YS - 1)) << 1) + (c ^ dc)


def vmem_call(kernel, out_shape, scalars, *arrays):
    smem = pl.BlockSpec(memory_space=pltpu.SMEM)
    vmem = pl.BlockSpec(memory_space=pltpu.VMEM)
    return pl.pallas_call(
        kernel,
        out_shape=out_shape,
        in_specs=[smem] * len(scalars) + [vmem] * len(arrays),
        out_specs=[vmem] * len(out_shape),
    )(*scalars, *arrays)


def split_kernel(keys, values, out):
    for h in range(KVH):
        out[h, 0] = keys[:, h * DH : (h + 1) * DH]
        out[h, 1] = values[:, h * DH : (h + 1) * DH]


def query_kernel(rank, queries, *parts):
    y, _, c = place(rank[0])
    for (dy, dc), part in zip(STEPS, parts, strict=True):
        column = pl.multiple_of(group_at(y, c, dy, dc) * GROUP, GROUP)
        part[...] = queries[:, pl.ds(column, GROUP)]


def attend_kernel(pieces, half, which, rank, doc_lengths, marks, *refs):
    parts = PARTS[which]
    part_refs, refs = refs[: len(parts)], refs[len(parts) :]
    q_refs, refs = refs[:pieces], refs[pieces:]
    if which == "far":
        acc_in, top_in, *refs = refs
    if which == "near":
        acc_out, top_out, *refs = refs
    else:
        o_refs, refs = refs[:pieces], refs[pieces:]
    q_all, o_all, acc, top, keys, values = refs
    rows = UNIT
    y, x, c = place(rank[0])

    for (dx, first_y, ys), part in zip(parts, part_refs, strict=True):
        at_x = (x + dx) & (XS - 1)
        for i in range(ys):
            for core in range(CS):
                block = first_y + i if which == "far" else (first_y + i) * XS + at_x
                at = pl.ds(pl.multiple_of((block * CS + core) * rows, rows), rows)
                keys[at, :] = part[i, core, 0]
                values[at, :] = part[i, core, 1]
    for p in range(pieces):
        for h in range(QPK):
            q_all[p, h * rows : (h + 1) * rows, :DH] = q_refs[p][:, h * DH : (h + 1) * DH]

    def tile(p, start, first_key, size, hidden=0, at_row=None, fresh=False):
        if which == "near":
            total, peak = acc_out.at[p], top_out.at[p]
        else:
            total, peak = acc, top
        at_key = pl.ds(pl.multiple_of(first_key if at_row is None else at_row, UNIT), size)
        if at_row is None:
            mark = marks[at_key, :]
        else:
            at_marks = [first_key + i * XS * TAIL for i in range(size // TAIL)]
            mark = [marks[pl.ds(pl.multiple_of(at, TAIL), TAIL), :] for at in at_marks]
            mark = jnp.concatenate(mark, axis=0)
        k_tile = jnp.concatenate([keys[at_key, :], mark], axis=1)
        v_tile = jnp.concatenate([values[at_key, :], jnp.ones((size, DH), jnp.bfloat16)], axis=1)
        count = QPK * rows // STACK
        stacks = [slice(i * STACK, (i + 1) * STACK) for i in range(count)]

        def multiply(i):
            return lax.dot_general(
                q_all[p, stacks[i], :],
                k_tile,
                (((1,), (1,)), ((), ())),
                preferred_element_type=jnp.float32,
            )

        def weigh(i, scores):
            if hidden:
                ahead = first_key + size - hidden - start
                q_row = lax.broadcasted_iota(jnp.int32, (STACK, hidden), 0) % rows - ahead
                keep = lax.broadcasted_iota(jnp.int32, (STACK, hidden), 1) <= q_row
                last = jnp.where(keep, scores[:, size - hidden :], NEG_FILL)
                if hidden == size:
                    scores = last
                else:
                    scores = jnp.concatenate([scores[:, : size - hidden], last], axis=1)
            new = jnp.max(scores, axis=1, keepdims=True)
            if fresh:
                new = jnp.broadcast_to(new, (STACK, DH))
            else:
                old = peak[stacks[i], :]
                new = jnp.maximum(old, new)
            weights = jnp.exp2((scores - jnp.tile(new, (1, size // DH))) * LOG2_SCALE)
            peak[stacks[i], :] = new
            rescale = None if fresh else jnp.exp2((old - new) * LOG2_SCALE)
            return weights.astype(jnp.bfloat16), rescale

        def add(i, weights, rescale):
            summed = jnp.dot(weights, v_tile, preferred_element_type=jnp.float32)
            if not fresh:
                summed = total[stacks[i], :] * jnp.tile(rescale, (1, 2)) + summed
            total[stacks[i], :] = summed

        coming, ready = multiply(0), None
        for i in range(count):
            scores = coming
            if i + 1 < count:
                coming = multiply(i + 1)
            weighed = weigh(i, scores)
            if ready is not None:
                add(i - 1, *ready)
            ready = weighed
        add(count - 1, *ready)

    @pl.loop(0, pieces)
    def _(p):
        dc = jnp.where(p == 0, 1 - half, half)
        start = ((((y - p) & (YS - 1)) * XS + x) * CS + (c ^ dc)) * rows

        def document(d, so_far):
            first, end = so_far
            after = end + doc_lengths[d]
            return jnp.where(end <= start, end, first), after

        first, _ = lax.fori_loop(0, doc_lengths.shape[0], document, (0, 0), unroll=True)
        mark = marks[pl.ds(pl.multiple_of(start, UNIT), rows), :]
        for h in range(QPK):
            q_all[p, h * rows : (h + 1) * rows, DH:] = mark + mark

        if which == "far":
            top[...] = top_in[p]
            acc[...] = acc_in[p]

            at_x = (x + 2) & (XS - 1)
            begin = jnp.maximum(first // TAIL - at_x + XS - 1, 0) // XS
            end = jnp.maximum(start // TAIL - at_x + XS - 1, 0) // XS
            count = jnp.maximum(end - begin, 0)

            @pl.loop(0, count // 2)
            def _(t):
                key = ((begin + 2 * t) * XS + at_x) * TAIL
                tile(p, start, key, 2 * TAIL, at_row=(begin + 2 * t) * TAIL)

            @pl.when(count % 2 == 1)
            def _():
                tile(p, start, ((end - 1) * XS + at_x) * TAIL, TAIL, at_row=(end - 1) * TAIL)

        else:
            lo, hi = first // UNIT, start // UNIT + 1
            tail, wide = TAIL // UNIT, WIDE // UNIT
            block = start // TAIL
            low = jnp.maximum(lo, tail * (block - 1)) if which == "near" else lo
            rest = jnp.maximum(hi - tail - low, 0)
            if which == "all":
                short = (wide - rest % wide) % wide
                rest = rest + jnp.where((short <= tail) & (short <= low), short, 0)
                low = jnp.maximum(hi - tail - rest, 0)
            odd = rest % tail
            begin = low + odd
            wides = (rest - odd) // wide

            @pl.when(hi - lo > 1)
            def _():
                tile(p, start, (hi - tail) * UNIT, TAIL, UNIT, fresh=True)

            @pl.when(hi - lo == 1)
            def _():
                tile(p, start, lo * UNIT, UNIT, UNIT, fresh=True)

            @pl.when(odd == 1)
            def _():
                tile(p, start, low * UNIT, UNIT)

            if which == "all":

                @pl.loop(0, wides)
                def _(t):
                    tile(p, start, (begin + t * wide) * UNIT, WIDE)

                left = (rest - odd - wides * wide) // tail

                @pl.loop(0, left // 2)
                def _(t):
                    tile(p, start, (begin + wides * wide + t * 2 * tail) * UNIT, 2 * TAIL)

                @pl.when(left % 2 == 1)
                def _():
                    tile(p, start, (hi - 2 * tail) * UNIT, TAIL)

            else:
                @pl.loop(0, jnp.where(rest > odd, 1, 0))
                def _(t):
                    tile(p, start, begin * UNIT, TAIL)

                @pl.loop(0, YS - 1)
                def _(n):
                    end = block + 2 - XS * (n + 1)
                    count = jnp.clip(end - jnp.maximum(lo // tail, 0), 0, NEAR_RUN)

                    @pl.when(count == NEAR_RUN)
                    def _():
                        tile(p, start, (end - NEAR_RUN) * TAIL, NEAR_RUN * TAIL)

                    @pl.when(count == 2)
                    def _():
                        tile(p, start, (end - 2) * TAIL, 2 * TAIL)

                    @pl.when(count == 1)
                    def _():
                        tile(p, start, (end - 1) * TAIL, TAIL)

        if which != "near":
            for h in range(QPK):
                at = slice(h * rows, (h + 1) * rows)
                result = acc[at, :DH] / acc[at, DH:]
                o_all[p, :, h * DH : (h + 1) * DH] = result.astype(jnp.bfloat16)

    if which != "near":
        for p in range(pieces):
            o_refs[p][...] = o_all[p]


def attend(half, which, rank, doc_lengths, marks, parts, q_pieces, state=()):
    pieces = len(q_pieces)
    seq = marks.shape[0]
    held = seq // XS if which == "far" else seq
    stacked = QPK * UNIT
    vmem = pl.BlockSpec(memory_space=pltpu.VMEM)
    smem = pl.BlockSpec(memory_space=pltpu.SMEM)
    if which == "near":
        out_shape = [
            jax.ShapeDtypeStruct((pieces, stacked, 2 * DH), jnp.float32),
            jax.ShapeDtypeStruct((pieces, stacked, DH), jnp.float32),
        ]
    else:
        out_shape = [jax.ShapeDtypeStruct((UNIT, GROUP), jnp.bfloat16)] * pieces
    return pl.pallas_call(
        functools.partial(attend_kernel, pieces, half, which),
        out_shape=out_shape,
        in_specs=[smem] * 2 + [vmem] * (1 + len(parts) + pieces + len(state)),
        out_specs=[vmem] * len(out_shape),
        scratch_shapes=[
            pltpu.VMEM((pieces, stacked, 2 * DH), jnp.bfloat16),
            pltpu.VMEM((pieces, UNIT, GROUP), jnp.bfloat16),
            pltpu.VMEM((stacked, 2 * DH), jnp.float32),
            pltpu.VMEM((stacked, DH), jnp.float32),
            pltpu.VMEM((held, DH), jnp.bfloat16),
            pltpu.VMEM((held, DH), jnp.bfloat16),
        ],
        compiler_params=pltpu.CompilerParams(vmem_limit_bytes=22 * 1024 * 1024),
        cost_estimate=pl.CostEstimate(
            flops=pieces * 4 * stacked * seq // 4 * DH,
            bytes_accessed=8 * 1024 * 1024,
            transcendentals=pieces * stacked * seq // 4,
        ),
    )(rank, doc_lengths, marks, *parts, *q_pieces, *state)


def per_device(queries, keys, values, doc_lengths):
    rows = queries.shape[0]
    seq = rows * YS * XS * CS
    rank = lax.axis_index("ctx").astype(jnp.int32)
    y, x, c = place(rank)
    rank = rank[None]

    by_head = jax.ShapeDtypeStruct((KVH, 2, rows, DH), jnp.bfloat16)
    (pairs,) = vmem_call(split_kernel, [by_head], (), keys, values)
    own = lax.all_to_all(
        pairs, "ctx", split_axis=0, concat_axis=0, tiled=True, axis_index_groups=head_groups()
    ).reshape(YS, CS, 2, rows, DH)
    doc_lengths, queries, own = lax.optimization_barrier((doc_lengths, queries, own))

    def along(part, dx):
        return lax.ppermute(part, "ctx", shift(0, dx, 0))

    left, right = along(own, 1), along(own, XS - 1)

    by_device = [jax.ShapeDtypeStruct((rows, GROUP), jnp.bfloat16)] * len(STEPS)
    sent = vmem_call(query_kernel, by_device, (rank,), queries)
    sent = dict(zip(STEPS, sent, strict=True))

    def send(dy, dc):
        part = sent[dy, dc]
        return lax.ppermute(part, "ctx", shift(dy, 0, dc)) if dy or dc else part

    first_half, second_half = STEPS[:YS], STEPS[YS:]
    got = {(0, 1): send(0, 1)}
    sent, got = lax.optimization_barrier((sent, got))
    got |= {step: send(*step) for step in first_half if step not in got}
    sent, got = lax.optimization_barrier((sent, got))
    got |= {step: send(*step) for step in second_half}
    some = YS // 2
    far = (along(left[:some], 1), along(right[some:], XS - 1))

    doc_end = jnp.cumsum(doc_lengths)
    none = jnp.zeros((DH - doc_end.shape[0],), jnp.int32)
    doc_first = jnp.concatenate([doc_end - doc_lengths, none])
    doc_end = jnp.concatenate([doc_end, none])
    positions = jnp.arange(seq, dtype=jnp.int32)[:, None]
    inside = (doc_first[None, :] <= positions) & (positions < doc_end[None, :])
    marks = jnp.where(inside, MARK, 0.0).astype(jnp.bfloat16)

    near = (own, left, right)
    pieces = [got[step] for step in first_half]
    state = attend(0, "near", rank, doc_lengths, marks, near, pieces)
    done = attend(0, "far", rank, doc_lengths, marks, far, pieces, state)

    def give(done, steps):
        return [
            lax.ppermute(piece, "ctx", shift(YS - dy, 0, dc)) if dy or dc else piece
            for (dy, dc), piece in zip(steps, done, strict=True)
        ]

    done, got = lax.optimization_barrier((done, got))
    outs = give(done, first_half)
    pieces = [got[step] for step in second_half]
    done = attend(1, "all", rank, doc_lengths, marks, near + far, pieces)
    in_chip, *across = outs
    done, across = lax.optimization_barrier((done, across))
    outs = [in_chip, *across, *give(done, second_half)]

    whole = jnp.zeros((rows, H * DH), jnp.bfloat16)
    for (dy, dc), piece in zip(STEPS, outs, strict=True):
        column = group_at(y, c, dy, dc) * GROUP
        whole = lax.dynamic_update_slice(
            whole, piece, (0, column), allow_negative_indices=False
        )
    return whole


def solution(mesh):
    placed = (P(("dp", "ctx"), None), P(("dp", "ctx"), None), P(("dp", "ctx"), None), P("dp"))
    return jax.shard_map(
        per_device, mesh=mesh, in_specs=placed, out_specs=P(("dp", "ctx"), None), check_vma=False
    )
```
